32 devices in a mesh: batch: 2 (over core), chan: 16 (over z, y, x).
Axes of the slice: x: 2, y: 2, z: 4, core: 2. Of those that a mesh axis runs over, the one named last changes fastest.
Arguments:
- inputs: bfloat16 [160, 24, 24, 384], P('batch', None, None, 'chan'), may hold values from -6 to 6
- valid_mask: int32 [160, 24, 24], P('batch'), may hold values from 0 to 1, as said below
- keep_mask: int32 [160], P('batch'), may hold values 0 or 1
- kernel: bfloat16 [7, 7, 384], P(None, None, 'chan'), may hold values from -0.875 to 0.875
- offset: bfloat16 [384], P('chan'), may hold values from -3 to 3
- norm_gain: bfloat16 [384], replicated, may hold values from 0.5 to 1.5
- norm_shift: bfloat16 [384], replicated, may hold values from -2 to 2
- expand_weight: bfloat16 [384, 1536], replicated, may hold values from -0.3125 to 0.3125
- expand_offset: bfloat16 [1536], replicated, may hold values from -3 to 3
- reduce_weight: bfloat16 [1536, 384], replicated, may hold values from -0.15625 to 0.15625
- reduce_offset: bfloat16 [384], replicated, may hold values from -3 to 3
- layer_scale: bfloat16 [384], replicated, may hold values from 0.5 to 2
- cotangent: bfloat16 [160, 24, 24, 384], P('batch', None, None, 'chan'), may hold values from -6 to 6
Outputs:
- block_output: bfloat16 [160, 24, 24, 384], P('batch', None, None, 'chan')
- input_gradient: bfloat16 [160, 24, 24, 384], P('batch', None, None, 'chan')
- kernel_gradient: float32 [7, 7, 384], P(None, None, 'chan')
- offset_gradient: float32 [384], P('chan')
- gain_gradient: float32 [384], replicated
- shift_gradient: float32 [384], replicated
- expand_gradient: float32 [384, 1536], replicated
- widen_gradient: float32 [1536], replicated
- reduce_gradient: float32 [1536, 384], replicated
- narrow_gradient: float32 [384], replicated
- scale_gradient: float32 [384], replicated
The draws below stay inside these ranges and needn't reach their ends.
Inputs may be any that keep to these rules, and one draw needn't show every extreme that they name: `valid_mask`: each image's valid pixels form the top-left square of side 14, 18 or 24 of its map.
All inputs are finite; a program needn't handle non-finite values. No bound on the sum of `keep_mask` on one device may be relied on, other than what follows from the above.
Results may differ from the reference program's by a relative error of at most 0.008.
Values may be sent and summed in bfloat16 or wider, within the bound.
A program may use at most 192 MiB of HBM per device.

```python
import math
import jax
import jax.numpy as jnp
from jax import lax

C = 384
FF = 1536
KS = 7
SIDE = 24
IMAGES = 160


def draw_valid_mask(key, part):
    key = jax.random.fold_in(key, 11)
    picked = jax.random.randint(key, (IMAGES,), 0, 3)
    border = jnp.where(picked == 0, 14, jnp.where(picked == 1, 18, SIDE))
    places = jnp.arange(SIDE)
    inside = (places[None, :, None] < border[:, None, None]) & (places[None, None, :] < border[:, None, None])
    return inside.astype(jnp.int32)


def plant(entries, key, low, largest):
    shape = entries.shape
    spot = [jax.random.randint(jax.random.fold_in(key, axis), (), 0, shape[axis]) for axis in range(len(shape))]
    entries = entries.at[tuple(spot)].set(low)
    longest = shape.index(max(shape))
    spot[longest] = (spot[longest] + 1) % shape[longest]
    return entries.at[tuple(spot)].set(largest)


def level_of(key, dims, pieces, least, high):
    def one(dim, blocks):
        heights = jax.random.uniform(jax.random.fold_in(jax.random.fold_in(key, 6), dim), (blocks,), jnp.float32, least / len(pieces), high / len(pieces))
        return jnp.repeat(jnp.exp(heights), dims[dim] // blocks).reshape((-1,) + (1,) * (len(dims) - dim - 1))

    level = one(*pieces[0])
    for cut in pieces[1:]:
        level = level * one(*cut)
    return level


def centred(stream_key, shape, scale, most, cuts=(), kind=jnp.bfloat16):
    factor_of = level_of(stream_key, shape, cuts, -0.22, 0.18) if cuts else 1.0
    drawn = jax.random.normal(stream_key, shape, jnp.float32) * scale * factor_of
    return jnp.minimum(jnp.maximum(drawn, -most), most).astype(kind)


def setup_inputs(seed: int = 0) -> dict:
    key_of = jax.random.split(jax.random.key(seed), 14)
    return {
        "inputs": centred(key_of[0], (IMAGES, SIDE, SIDE, C), 1.0, 6.0, ((0, 2), (3, 16))),
        "valid_mask": draw_valid_mask(jax.random.fold_in(key_of[13], 71), 0),
        "keep_mask": plant((jax.random.randint(key_of[2], (IMAGES,), 0, 10) < 9).astype(jnp.int32), jax.random.fold_in(key_of[2], 1), 0, 1),
        "kernel": centred(key_of[3], (KS, KS, C), (KS * KS) ** -0.5, 0.875, ((2, 16),)),
        "offset": centred(key_of[4], (C,), 0.5, 3.0, ((0, 16),)),
        "norm_gain": jnp.clip(1.0 + 0.1 * jax.random.normal(key_of[5], (C,), jnp.float32), 0.5, 1.5).astype(jnp.bfloat16),
        "norm_shift": centred(key_of[6], (C,), 0.3, 2.0),
        "expand_weight": centred(key_of[7], (C, FF), C ** -0.5, 0.3125),
        "expand_offset": centred(key_of[8], (FF,), 0.5, 3.0),
        "reduce_weight": centred(key_of[9], (FF, C), FF ** -0.5, 0.15625),
        "reduce_offset": centred(key_of[10], (C,), 0.5, 3.0),
        "layer_scale": jnp.clip(jnp.exp(jax.random.uniform(key_of[11], (C,), jnp.float32, math.log(0.5), math.log(2.0))), 0.5, 2.0).astype(jnp.bfloat16),
        "cotangent": centred(key_of[12], (IMAGES, SIDE, SIDE, C), 1.0, 6.0, ((0, 2), (3, 16))),
    }


@jax.custom_vjp
def low(v):
    return lax.optimization_barrier(v.astype(jnp.bfloat16)).astype(jnp.float32)

@jax.custom_vjp
def low_back(v):
    return v

def low_keep(v):
    return (low(v), None)

def low_pass(kept, grad):
    return (grad,)

def back_keep(v):
    return (v, None)

def back_low(kept, grad):
    return (low(grad),)
low.defvjp(low_keep, low_pass)
low_back.defvjp(back_keep, back_low)
keep_rate = 0.9
epsilon = 1e-06

def exact_gelu(values):
    return jax.nn.gelu(values, approximate=False)

def depthwise(masked, kern):
    reach = KS // 2
    padded = jnp.pad(masked, ((0, 0), (reach, reach), (reach, reach), (0, 0)))
    total = jnp.zeros(masked.shape, masked.dtype)
    for row in range(KS):
        for column in range(KS):
            total = total + padded[:, row:row + SIDE, column:column + SIDE, :] * kern[row, column]
    return total

def reference(inputs, valid_mask, keep_mask, kernel, offset, norm_gain, norm_shift, expand_weight, expand_offset, reduce_weight, reduce_offset, layer_scale, cotangent):
    mask_f = valid_mask.astype(jnp.float32)[..., None]
    factor = mask_f * (keep_mask.astype(jnp.float32) / keep_rate)[:, None, None, None]
    per_block = 8 if IMAGES % 8 == 0 else 4 if IMAGES % 4 == 0 else 2 if IMAGES % 2 == 0 else 1
    count = IMAGES // per_block
    mask_blocks = mask_f.reshape(count, per_block, SIDE, SIDE, 1)
    factor_blocks = factor.reshape(count, per_block, SIDE, SIDE, 1)

    def forward(source, kern, bias, gain, shift, expand, widen, reduce_w, narrow, scale):
        source_blocks = source.reshape(count, per_block, SIDE, SIDE, C)

        def one_block(items):
            rows, mask_here, factor_here = items
            conv = depthwise(rows * mask_here, kern)
            filtered = low(low_back((conv + bias) * mask_here)).reshape(per_block * SIDE * SIDE, C)
            center = lax.optimization_barrier(jnp.mean(filtered, axis=-1, keepdims=True))
            spread = lax.optimization_barrier(jnp.mean(jnp.square(filtered - center), axis=-1, keepdims=True))
            normed = low((filtered - center) * lax.rsqrt(spread + epsilon) * gain + shift)
            hidden = low_back(jnp.dot(normed, expand, precision=lax.Precision.HIGHEST) + widen)
            active = low(exact_gelu(hidden))
            reduced = low_back(jnp.dot(active, reduce_w, precision=lax.Precision.HIGHEST) + narrow)
            branch = low(low_back(scale * reduced)).reshape(rows.shape)
            return rows + factor_here * branch
        outputs = lax.map(jax.checkpoint(one_block), (source_blocks, mask_blocks, factor_blocks))
        return outputs.reshape(source.shape)
    primals = (inputs, kernel, offset, norm_gain, norm_shift, expand_weight, expand_offset, reduce_weight, reduce_offset, layer_scale)
    primals = tuple((p.astype(jnp.float32) for p in primals))
    output, pullback = jax.vjp(forward, *primals)
    grads = pullback(cotangent.astype(jnp.float32))
    return (output.astype(jnp.bfloat16), grads[0].astype(jnp.bfloat16), grads[1], grads[2], grads[3], grads[4], grads[5], grads[6], grads[7], grads[8], grads[9])
```

```python
import functools
import numpy as np
import jax
import jax.numpy as jnp
from jax import lax
from jax.experimental import pallas as pl
from jax.experimental.pallas import tpu as pltpu
from jax.sharding import PartitionSpec as P

F32, BF16, I32 = jnp.float32, jnp.bfloat16, jnp.int32
MESH = pl.DeviceIdType.MESH
L = 128
FACTOR = np.float32(1.0) / np.float32(0.9)
CH = 2
SIZES = (14, 16)


def gelu_parts(h):
    x = jnp.abs(h)
    a = 1.0 + np.float32(0.3275911 / np.sqrt(2.0)) * x
    t = pl.reciprocal(a, approx=True)
    t = t * (2.0 - a * t)
    e = jnp.exp(-0.5 * h * h)
    c = [0.5 * v for v in (0.254829592, -0.284496736, 1.421413741, -1.453152027, 1.061405429)]
    poly = t * (c[0] + t * (c[1] + t * (c[2] + t * (c[3] + t * c[4]))))
    q = poly * e
    cdf = jnp.where(h >= 0, 1.0 - q, q)
    return h * cdf, cdf + (np.float32(1 / np.sqrt(2 * np.pi)) * h) * e


def main_kernel(cfg, plo, off, x_ref, s_ref, cot_ref, perm_ref, taps_ref, bias_ref, band_ref,
                w1_ref, w1t_ref, w2_ref, w2t_ref, cols_ref, b1_ref,
                fc_out, br_out, xpad_out, rg_out, eg_out, small_out,
                xf, srt, xpad, bc_send, f_send, bc_recv, f_recv, fc_send, br_send,
                rg_acc, eg_acc, vec_acc, wid_acc, res, hold, small, small_recv,
                in_ssem, in_rsem, out_ssem, out_rsem, cp_sem, ex_ssem, ex_rsem, sm_ssem, sm_rsem):
    side, C, N, K, NC, T = cfg
    C2 = NC * C
    FF = w1t_ref.shape[0]
    rows = side * C
    b = lax.axis_index("batch")
    me = lax.axis_index("chan")

    bar = pltpu.get_barrier_semaphore()
    def greet(m, _):
        pl.semaphore_signal(bar, inc=1, device_id=(b, lax.rem(me + m, NC)), device_id_type=MESH)
        return 0
    lax.fori_loop(1, NC, greet, 0)
    pl.semaphore_signal(bar, inc=1, device_id=(1 - b, me), device_id_type=MESH)
    pl.semaphore_wait(bar, NC)

    lane = lax.broadcasted_iota(I32, (C, L), 1)
    perm = perm_ref[...]
    s = s_ref[...]

    def send(src, dst, k, ssem, rsem):
        sl = pl.ds(k * CH, CH)
        def one(m, _):
            t = lax.rem(me + m, NC)
            pltpu.make_async_remote_copy(
                src_ref=src.at[sl, t], dst_ref=dst.at[sl, me], send_sem=ssem, recv_sem=rsem,
                device_id=(b, t), device_id_type=MESH).start()
            return 0
        lax.fori_loop(1, NC, one, 0)
        pltpu.make_async_copy(src.at[sl, me], dst.at[sl, me], rsem).start()

    def arrived(dst, k, rsem):
        ref = dst.at[pl.ds(k * CH, CH)]
        pltpu.make_async_copy(ref, ref, rsem).wait()

    def sent(src, ssem):
        ref = src.at[:, pl.ds(0, NC - 1)]
        pltpu.make_async_copy(ref, ref, ssem).wait()

    def pack(dst, k):
        def group(g):
            p0 = plo[g]
            acc = jnp.zeros((C, L), F32)
            for t in range(T):
                sh = off[p0 + t] - g * L
                v = srt[p0 + t]
                acc = jnp.where(lane >= sh, pltpu.roll(v, lax.bitwise_and(sh, L - 1), 1), acc)
            return acc
        B = 8
        def body(h, _):
            s0 = k * CH + h * B // NC
            d0 = lax.rem(h * B, NC)
            accs = [group(s0 * NC + d0 + i) for i in range(B)]
            for i in range(B):
                dst[s0, d0 + i] = accs[i].astype(BF16)
            return 0
        lax.fori_loop(0, CH * NC // B, body, 0, unroll=2)

    srt[side * side] = jnp.zeros((C, L), F32)
    def bc_row(i, _):
        parts = []
        for j in range(side):
            m = jnp.where(s > jnp.maximum(i, j), FACTOR, F32(0.0))
            parts.append(cot_ref[i, j].astype(F32) * m)
        v = jnp.concatenate(parts, axis=0).astype(BF16)
        srt[pl.ds(i * side, side)] = jnp.dot(v, perm_ref[0:N, :], preferred_element_type=F32).reshape(side, C, L)
        return 0
    lax.fori_loop(0, side, bc_row, 0)
    def bc_chunk(k, _):
        pack(bc_send, k)
        send(bc_send, bc_recv, k, in_ssem.at[0], in_rsem.at[0, k])
        return 0
    lax.fori_loop(0, K // CH, bc_chunk, 0)

    def x_row(i, _):
        for j in range(side):
            m = (s > jnp.maximum(i, j)).astype(F32)
            xf[pl.ds(pl.multiple_of(i * rows + j * C, 8), C), 0:N] = x_ref[i, j].astype(F32) * m
        return 0
    lax.fori_loop(0, side, x_row, 0)
    xpad[...] = jnp.zeros_like(xpad)

    def channel(c, _):
        xpad[c, 96:96 + 576, 0:N] = xf[pl.ds(c, 576, stride=C), :][:, 0:N].astype(BF16)
        tap = jnp.broadcast_to(taps_ref[pl.ds(c, 1), :], (8, 384))
        tiles = [pltpu.roll(tap, 8 * k, 1, stride=1, stride_axis=0) * band_ref[8 * k:8 * k + 8, :] for k in range(24)]
        toep = jnp.concatenate(tiles, axis=0).astype(BF16)
        win = jnp.concatenate([xpad[c, 192 * g:192 * g + 384, :] for g in range(3)], axis=1)
        out = jnp.dot(toep, win, preferred_element_type=F32)
        for g in range(3):
            xf[pl.ds(g * 192 * C + c, 192, stride=C), :] = out[:, g * L:(g + 1) * L]
        return 0
    lax.fori_loop(0, C, channel, 0)
    xcopy = pltpu.make_async_copy(xpad, xpad_out, cp_sem)
    xcopy.start()

    bias = jnp.concatenate([bias_ref[...]] * side, axis=0)
    def f_row(i, _):
        r = pl.ds(pl.multiple_of(i * rows, 8), rows)
        v = (xf[r, :] + bias).astype(BF16)
        srt[pl.ds(i * side, side)] = jnp.dot(v, perm, preferred_element_type=F32).reshape(side, C, L)
        return 0
    lax.fori_loop(0, side, f_row, 0)
    def f_chunk(k, _):
        pack(f_send, k)
        send(f_send, f_recv, k, in_ssem.at[1], in_rsem.at[1, k])
        return 0
    lax.fori_loop(0, K // CH, f_chunk, 0)

    rg_acc[...] = jnp.zeros_like(rg_acc)
    eg_acc[...] = jnp.zeros_like(eg_acc)
    vec_acc[...] = jnp.zeros_like(vec_acc)
    wid_acc[...] = jnp.zeros_like(wid_acc)
    W = CH * L
    FB = 256
    NT = (((1,), (1,)), ((), ()))

    def fold(v):
        out = v[:, 0:L]
        for t in range(1, CH):
            out = out + v[:, t * L:(t + 1) * L]
        return out

    def load(ref, k):
        return jnp.concatenate([ref[k * CH + t].astype(F32).reshape(C2, L) for t in range(CH)], axis=1)

    def store(ref, k, v):
        for t in range(CH):
            ref[k * CH + t] = v[:, t * L:(t + 1) * L].reshape(NC, C, L).astype(BF16)

    def mlp(k, _):
        arrived(bc_recv, k, in_rsem.at[0, k])
        arrived(f_recv, k, in_rsem.at[1, k])
        gain, shift, b2, scale = (cols_ref[:, i:i + 1] for i in range(4))
        f = load(f_recv, k)
        center = jnp.mean(f, axis=0, keepdims=True)
        d = f - center
        inv = lax.rsqrt(jnp.mean(d * d, axis=0, keepdims=True) + 1e-6)
        xhat = d * inv
        normed = (xhat * gain + shift).astype(BF16)
        bc = load(bc_recv, k)
        rcf = (scale * bc).astype(BF16)
        vec_acc[2] += fold(rcf.astype(F32))
        red = jnp.zeros((C2, W), F32)
        nc = jnp.zeros((C2, W), F32)
        for fb in range(FF // FB):
            r = slice(fb * FB, (fb + 1) * FB)
            h = jnp.dot(w1t_ref[r, :], normed, preferred_element_type=F32) + b1_ref[r, :]
            act, dg = gelu_parts(h)
            act = act.astype(BF16)
            ac = jnp.dot(w2_ref[r, :], rcf, preferred_element_type=F32)
            hc = (ac * dg).astype(BF16)
            red = red + jnp.dot(w2t_ref[:, r], act, preferred_element_type=F32)
            nc = nc + jnp.dot(w1_ref[:, r], hc, preferred_element_type=F32)
            rg_acc[r, :] += lax.dot_general(act, rcf, NT, preferred_element_type=F32)
            eg_acc[r, :] += lax.dot_general(hc, normed, NT, preferred_element_type=F32)
            wid_acc[r, :] += fold(hc.astype(F32))
        red = red + b2
        store(br_send, k, scale * red)
        vec_acc[3] += fold(bc * red)
        vec_acc[0] += fold(nc * xhat)
        vec_acc[1] += fold(nc)
        q = nc * gain
        m1 = jnp.mean(q, axis=0, keepdims=True)
        m2 = jnp.mean(q * xhat, axis=0, keepdims=True)
        store(fc_send, k, inv * (q - m1 - xhat * m2))
        send(fc_send, fc_out, k, out_ssem.at[0], out_rsem.at[0, k])
        return 0
    lax.fori_loop(0, K // CH, mlp, 0)
    def br_chunk(k, _):
        send(br_send, br_out, k, out_ssem.at[1], out_rsem.at[1, k])
        return 0
    lax.fori_loop(0, K // CH, br_chunk, 0)

    ones = jnp.ones((8, L), F32)
    def row_of(v):
        return lax.dot_general(ones, v, NT, precision=lax.Precision.HIGHEST, preferred_element_type=F32)
    sub = lax.broadcasted_iota(I32, (8, C2), 0)
    tot = jnp.zeros((8, C2), F32)
    for i in range(4):
        tot = tot + jnp.where(sub == i, row_of(vec_acc[i]), 0.0)
    for i in range(FF // C2):
        tot = tot + jnp.where(sub == 4 + i, row_of(wid_acc[i * C2:(i + 1) * C2, :]), 0.0)
    small[...] = tot

    xb, yb, zb = lax.rem(me, 2), lax.rem(me // 2, 2), me // 4
    accs = (rg_acc, eg_acc)
    base = [0, 0]
    span = FF
    def peer(bit):
        if bit == "c":
            return (1 - b, me), b
        if bit == "x":
            return (b, me + 1 - 2 * xb), xb
        return (b, me + 2 - 4 * yb), yb
    lo = 0
    steps = (("c", "c"), ("x", "y"), ("y", "x"))
    hist = []
    for st, bits in enumerate(steps):
        span //= 2
        cps = []
        for a in range(2):
            dev, bit = peer(bits[a])
            theirs = pl.multiple_of(base[a] + (1 - bit) * span, 16)
            mine = pl.multiple_of(base[a] + bit * span, 16)
            hold[a, lo:lo + span, :] = accs[a][pl.ds(theirs, span), :].astype(BF16)
            cp = pltpu.make_async_remote_copy(
                src_ref=hold.at[a, pl.ds(lo, span)], dst_ref=res.at[a, pl.ds(lo, span)],
                send_sem=ex_ssem.at[a, st], recv_sem=ex_rsem.at[a, st], device_id=dev, device_id_type=MESH)
            cp.start()
            cps.append(cp)
            hist.append((st, a, dev, base[a], mine))
            base[a] = mine
        dev, _ = peer(bits[0])
        sc = pltpu.make_async_remote_copy(
            src_ref=small, dst_ref=small_recv.at[st], send_sem=sm_ssem.at[st], recv_sem=sm_rsem.at[st],
            device_id=dev, device_id_type=MESH)
        sc.start()
        for a in range(2):
            cps[a].wait()
            accs[a][pl.ds(base[a], span), :] += res[a, lo:lo + span, :].astype(F32)
        sc.wait()
        small[...] += small_recv[st]
        lo += span
    Z = NC // 4
    span //= Z
    cps = []
    for m in range(1, Z):
        zt = lax.rem(zb + m, Z)
        dev = (b, me + 4 * (zt - zb))
        for a in range(2):
            theirs = pl.multiple_of(base[a] + zt * span, 16)
            hold[a, lo + (m - 1) * span:lo + m * span, :] = accs[a][pl.ds(theirs, span), :].astype(BF16)
            cp = pltpu.make_async_remote_copy(
                src_ref=hold.at[a, pl.ds(lo + (m - 1) * span, span)], dst_ref=res.at[a, pl.ds(lo + (m - 1) * span, span)],
                send_sem=ex_ssem.at[a, 2 + m], recv_sem=ex_rsem.at[a, 2 + m], device_id=dev, device_id_type=MESH)
            cp.start()
            cps.append(cp)
        cp = pltpu.make_async_remote_copy(
            src_ref=small, dst_ref=small_recv.at[3 + zb], send_sem=sm_ssem.at[2 + m], recv_sem=sm_rsem.at[2 + m],
            device_id=dev, device_id_type=MESH)
        cp.start()
        cps.append(cp)
    small_recv[3 + zb] = small[...]
    for cp in cps:
        cp.wait()
    own = []
    for a in range(2):
        mine = pl.multiple_of(base[a] + zb * span, 16)
        v = accs[a][pl.ds(mine, span), :]
        for m in range(1, Z):
            v = v + res[a, lo + (m - 1) * span:lo + m * span, :].astype(F32)
        own.append((mine, v))
    small_out[...] = sum(small_recv[3 + i] for i in range(1, Z)) + small_recv[3]
    outs = (rg_out, eg_out)
    for a in range(2):
        outs[a][pl.ds(own[a][0], span), :] = own[a][1].astype(BF16)
    cps = []
    for m in range(1, Z):
        zt = lax.rem(zb + m, Z)
        dev = (b, me + 4 * (zt - zb))
        for a in range(2):
            ref = outs[a].at[pl.ds(own[a][0], span)]
            cp = pltpu.make_async_remote_copy(
                src_ref=ref, dst_ref=ref, send_sem=ex_ssem.at[a, 5 + m], recv_sem=ex_rsem.at[a, 5 + m],
                device_id=dev, device_id_type=MESH)
            cp.start()
            cps.append(cp)
    for cp in cps:
        cp.wait()
    span *= Z
    for st in (2, 1, 0):
        cps = []
        for (h, a, dev, _, mine) in hist:
            if h == st:
                ref = outs[a].at[pl.ds(mine, span)]
                cp = pltpu.make_async_remote_copy(
                    src_ref=ref, dst_ref=ref, send_sem=ex_ssem.at[a, 9 + st], recv_sem=ex_rsem.at[a, 9 + st],
                    device_id=dev, device_id_type=MESH)
                cp.start()
                cps.append(cp)
        for cp in cps:
            cp.wait()
        span *= 2

    xcopy.wait()
    for k in range(K // CH):
        arrived(fc_out, k, out_rsem.at[0, k])
        arrived(br_out, k, out_rsem.at[1, k])
    sent(bc_send, in_ssem.at[0])
    sent(f_send, in_ssem.at[1])
    sent(fc_send, out_ssem.at[0])
    sent(br_send, out_ssem.at[1])


def tail_kernel(cfg, off, x_ref, s_ref, cot_ref, permt_ref, taps_ref, band_ref, xpad, fc_ref, br_ref,
                out_ref, ig_ref, kg_ref, og_ref, xf, cpad):
    side, C, N, K, NC, T = cfg
    rows = side * C
    lane = lax.broadcasted_iota(I32, (C, L), 1)
    s = s_ref[...]
    permt = permt_ref[...]

    def unpack(src, i, j):
        p = i * side + j
        o = off[p]
        g = lax.shift_right_logical(o, 7)
        r = lax.bitwise_and(o, L - 1)
        a = src[g].astype(F32)
        v = src[jnp.minimum(g + 1, src.shape[0] - 1)].astype(F32)
        v = jnp.where(lane >= r, a, v)
        v = pltpu.roll(v, lax.bitwise_and(L - r, L - 1), 1)
        m = jnp.maximum(i, j)
        n = jnp.where(m < 14, off[602], jnp.where(m < 18, off[601], off[600]))
        return jnp.where(lane < n, v, 0.0)

    og_ref[...] = jnp.zeros_like(og_ref)
    def fc_row(i, _):
        parts = [unpack(fc_ref, i, j) for j in range(side)]
        tot = parts[0]
        for p in parts[1:]:
            tot = tot + p
        og_ref[...] += tot
        v = jnp.concatenate(parts, axis=0).astype(BF16)
        xf[pl.ds(pl.multiple_of(i * rows, 8), rows), :] = jnp.dot(v, permt, preferred_element_type=F32)
        return 0
    lax.fori_loop(0, side, fc_row, 0)
    cpad[...] = jnp.zeros_like(cpad)
    NT = (((1,), (1,)), ((), ()))

    def channel(c, _):
        cpad[c, 96:96 + 576, :] = xf[pl.ds(c, 576, stride=C), :].astype(BF16)
        tap = jnp.broadcast_to(taps_ref[pl.ds(c, 1), :], (8, 384))
        tiles = [pltpu.roll(tap, 8 * k, 1, stride=1, stride_axis=0) * band_ref[8 * k:8 * k + 8, :] for k in range(24)]
        toep = jnp.concatenate(tiles, axis=0).astype(BF16)
        win = jnp.concatenate([cpad[c, 192 * g:192 * g + 384, :] for g in range(3)], axis=1)
        out = jnp.dot(toep, win, preferred_element_type=F32)
        for g in range(3):
            xf[pl.ds(g * 192 * C + c, 192, stride=C), :] = out[:, g * L:(g + 1) * L]
        cen = jnp.concatenate([cpad[c, 96 + 192 * g:288 + 192 * g, :] for g in range(3)], axis=1)
        xwin = jnp.concatenate([xpad[c, 192 * g:192 * g + 384, :] for g in range(3)], axis=1)
        gram = lax.dot_general(cen, xwin, NT, preferred_element_type=F32) * band_ref[...]
        acc = jnp.zeros((8, 384), F32)
        for k in range(24):
            acc = acc + pltpu.roll(gram[8 * k:8 * k + 8, :], (384 - 8 * k) % 384, 1)
        kg_ref[c] = acc
        return 0
    lax.fori_loop(0, C, channel, 0)

    def ig_row(i, _):
        for j in range(side):
            m = (s > jnp.maximum(i, j)).astype(F32)
            v = xf[pl.ds(pl.multiple_of(i * rows + j * C, 8), C), :][:, 0:N]
            ig_ref[i, j] = (cot_ref[i, j].astype(F32) + v * m).astype(BF16)
        return 0
    lax.fori_loop(0, side, ig_row, 0)

    def br_row(i, _):
        parts = [unpack(br_ref, i, j) for j in range(side)]
        v = jnp.concatenate(parts, axis=0).astype(BF16)
        v = jnp.dot(v, permt, preferred_element_type=F32)
        for j in range(side):
            out_ref[i, j] = (x_ref[i, j].astype(F32) + FACTOR * v[j * C:(j + 1) * C, 0:N]).astype(BF16)
        return 0
    lax.fori_loop(0, side, br_row, 0)


def plan(valid_mask, keep_mask, side, groups):
    wide = jnp.sum(valid_mask[:, 0, :], axis=1)
    key = jnp.where(keep_mask > 0, 1 + (wide >= 18).astype(I32) + (wide >= 24).astype(I32), 0)
    n = key.shape[0]
    idx = jnp.arange(n)
    ahead = (key[None, :] > key[:, None]) | ((key[None, :] == key[:, None]) & (idx[None, :] < idx[:, None]))
    rank = jnp.sum(ahead.astype(I32), axis=1)
    lanes = jnp.arange(L)
    perm = ((rank[:, None] == lanes[None, :]) & (key[:, None] > 0)).astype(BF16)
    permt = ((rank[None, :] == lanes[:, None]) & (key[None, :] > 0)).astype(BF16)
    perm = jnp.pad(perm, ((0, L - n), (0, 0)))
    permt = jnp.pad(permt, ((0, 0), (0, L - n)))
    counts = [jnp.sum((key >= t).astype(I32)) for t in (3, 2, 1)]
    strides = [jnp.maximum(c, 16) for c in counts]
    reach = np.maximum(*np.meshgrid(np.arange(side), np.arange(side), indexing="ij")).reshape(-1)
    group = [reach >= 18, (reach >= 14) & (reach < 18), reach < 14]
    before = [np.concatenate([[0], np.cumsum(m)]).astype(np.int32) for m in group]
    off = sum(strides[i] * before[i] for i in range(3))
    total = off[-1]
    ends = off[1:]
    plo = jnp.sum((ends[None, :] <= (jnp.arange(groups) * L)[:, None]).astype(I32), axis=1)
    fill = jnp.full((600 - off.shape[0],), 1 << 20, I32)
    off = jnp.concatenate([off, fill, jnp.stack(counts), jnp.zeros((5,), I32)])
    return wide, perm, permt, plo, off, total


def fast(K, cid, inputs, kernel, offset, norm_gain, norm_shift, expand_weight, expand_offset, reduce_weight, reduce_offset,
         layer_scale, cotangent, wide, perm, permt, plo, off):
    N, side, _, C = inputs.shape
    C2, FF = expand_weight.shape
    NC = C2 // C
    T = 9
    cfg = (side, C, N, K, NC, T)
    G = K * NC
    x = jnp.transpose(inputs, (1, 2, 3, 0))
    cot = jnp.transpose(cotangent, (1, 2, 3, 0))
    ks = kernel.shape[0]
    def taps_of(k):
        t = jnp.transpose(k.astype(F32), (2, 0, 1))
        t = jnp.pad(t, ((0, 0), (0, 0), (0, side - ks))).reshape(C, ks * side)
        return jnp.pad(t, ((0, 0), (21, 384 - 21 - ks * side)))
    r = np.arange(192)
    l = np.arange(384)
    band = (np.abs(l[None] % side - r[:, None] % side) <= 3).astype(np.float32)
    bias = jnp.broadcast_to(offset.astype(F32)[:, None], (C, L))
    cols = jnp.stack([norm_gain, norm_shift, reduce_offset, layer_scale], axis=1).astype(F32)
    b1 = expand_offset.astype(F32)[:, None]
    s = wide[None, :]
    vm = pl.BlockSpec(memory_space=pltpu.VMEM)
    sm = pl.BlockSpec(memory_space=pltpu.SMEM)
    anyspec = pl.BlockSpec(memory_space=pl.ANY)
    blk = (K, NC, C, L)
    Z = NC // 4
    res_rows = FF * 7 // 8 + (Z - 1) * (FF // 8 // Z)
    fc, br, xpad, rg, eg, small = pl.pallas_call(
        functools.partial(main_kernel, cfg),
        out_shape=[jax.ShapeDtypeStruct(blk, BF16)] * 2 + [jax.ShapeDtypeStruct((C, 768, L), BF16)]
        + [jax.ShapeDtypeStruct((FF, C2), BF16)] * 2 + [jax.ShapeDtypeStruct((8, C2), F32)],
        in_specs=[sm] * 2 + [vm] * 13,
        out_specs=[anyspec] * 3 + [vm] * 3,
        scratch_shapes=[
            pltpu.VMEM((side * side * C, L), F32), pltpu.VMEM((600, C, L), F32), pltpu.VMEM((C, 768, L), BF16),
            pltpu.VMEM(blk, BF16), pltpu.VMEM(blk, BF16), pltpu.VMEM(blk, BF16), pltpu.VMEM(blk, BF16),
            pltpu.VMEM(blk, BF16), pltpu.VMEM(blk, BF16),
            pltpu.VMEM((FF, C2), F32), pltpu.VMEM((FF, C2), F32), pltpu.VMEM((4, C2, L), F32), pltpu.VMEM((FF, L), F32),
            pltpu.VMEM((2, res_rows, C2), BF16), pltpu.VMEM((2, res_rows, C2), BF16),
            pltpu.VMEM((8, C2), F32), pltpu.VMEM((3 + Z, 8, C2), F32),
            pltpu.SemaphoreType.DMA((2,)), pltpu.SemaphoreType.DMA((2, K // CH)),
            pltpu.SemaphoreType.DMA((2,)), pltpu.SemaphoreType.DMA((2, K // CH)),
            pltpu.SemaphoreType.DMA,
            pltpu.SemaphoreType.DMA((2, 12)), pltpu.SemaphoreType.DMA((2, 12)),
            pltpu.SemaphoreType.DMA((6,)), pltpu.SemaphoreType.DMA((6,)),
        ],
        compiler_params=pltpu.CompilerParams(collective_id=cid, has_side_effects=True, vmem_limit_bytes=60 << 20),
        name="main_k%d" % K,
    )(plo, off, x, s, cot, perm, taps_of(kernel), bias, band, expand_weight, expand_weight.T, reduce_weight, reduce_weight.T, cols, b1)
    img = jax.ShapeDtypeStruct((side, side, C, N), BF16)
    out, ig, kg, og = pl.pallas_call(
        functools.partial(tail_kernel, cfg),
        out_shape=[img, img, jax.ShapeDtypeStruct((C, 8, 384), F32), jax.ShapeDtypeStruct((C, L), F32)],
        in_specs=[sm] + [vm] * 9, out_specs=[vm] * 4,
        scratch_shapes=[pltpu.VMEM((600 * C, L), F32), pltpu.VMEM((C, 768, L), BF16)],
        compiler_params=pltpu.CompilerParams(vmem_limit_bytes=60 << 20),
        name="tail_k%d" % K,
    )(off, x, s, cot, permt, taps_of(kernel[::-1, ::-1]), band, xpad, fc.reshape(G, C, L), br.reshape(G, C, L))
    kg = sum(kg[:, q, 21 + q:21 + q + ks * side] for q in range(8))
    kg = jnp.transpose(kg.reshape(C, ks, side)[:, :, :ks], (1, 2, 0))
    kg, og = lax.psum((kg, jnp.sum(og, axis=1)), "batch")
    return (jnp.transpose(out, (3, 0, 1, 2)), jnp.transpose(ig, (3, 0, 1, 2)), kg, og, small[0], small[1],
            eg.T.astype(F32), small[4:].reshape(-1), rg.astype(F32), small[2], small[3])


keep_rate = 0.9
epsilon = 1e-06


def exact_gelu(values):
    return jax.nn.gelu(values, approximate=False)


def layer_norm(values, gain, shift):
    center = jnp.mean(values, axis=-1, keepdims=True)
    spread = jnp.mean(jnp.square(values - center), axis=-1, keepdims=True)
    return (values - center) * lax.rsqrt(spread + epsilon) * gain + shift


def dense_form(
    inputs,
    valid_mask,
    keep_mask,
    kernel,
    offset,
    norm_gain,
    norm_shift,
    expand_weight,
    expand_offset,
    reduce_weight,
    reduce_offset,
    layer_scale,
    cotangent,
):
    images, height, breadth, channels = inputs.shape
    kside = kernel.shape[0]
    pixels = images * height * breadth
    mask_f = valid_mask.astype(jnp.float32)
    factor = mask_f * (keep_mask.astype(jnp.float32) / keep_rate)[:, None, None]

    def local_conv(source, kern):
        return lax.conv_general_dilated(
            source,
            kern.reshape(kside, kside, 1, channels),
            (1, 1),
            "SAME",
            dimension_numbers=("NHWC", "HWIO", "NHWC"),
            feature_group_count=channels,
            precision=lax.Precision.HIGHEST,
        )

    masked = inputs.astype(jnp.float32) * mask_f[..., None]
    conv_out, conv_pull = jax.vjp(local_conv, masked, kernel.astype(jnp.float32))
    filtered = ((conv_out + offset.astype(jnp.float32)) * mask_f[..., None]).astype(jnp.bfloat16)
    flat_filtered = filtered.reshape(pixels, channels)
    pixel_rows = lax.all_to_all(flat_filtered, "chan", split_axis=0, concat_axis=1, tiled=True)
    normed_f, norm_pull = jax.vjp(
        layer_norm,
        pixel_rows.astype(jnp.float32),
        norm_gain.astype(jnp.float32),
        norm_shift.astype(jnp.float32),
    )
    normed = normed_f.astype(jnp.bfloat16)
    hidden = jnp.dot(
        normed, expand_weight, preferred_element_type=jnp.float32
    ) + expand_offset.astype(jnp.float32)
    active_f, gelu_pull = jax.vjp(exact_gelu, hidden)
    active = active_f.astype(jnp.bfloat16)
    reduced = jnp.dot(
        active, reduce_weight, preferred_element_type=jnp.float32
    ) + reduce_offset.astype(jnp.float32)
    scale_f = layer_scale.astype(jnp.float32)
    branch = (scale_f * reduced).astype(jnp.bfloat16)
    branch_back = lax.all_to_all(branch, "chan", split_axis=1, concat_axis=0, tiled=True)
    block_output = inputs.astype(jnp.float32) + factor[..., None] * branch_back.reshape(
        inputs.shape
    ).astype(jnp.float32)
    local_cot = (
        (cotangent.astype(jnp.float32) * factor[..., None])
        .astype(jnp.bfloat16)
        .reshape(pixels, channels)
    )
    branch_cot = lax.all_to_all(local_cot, "chan", split_axis=0, concat_axis=1, tiled=True)
    branch_cot_f = branch_cot.astype(jnp.float32)
    scale_sum = jnp.sum(branch_cot_f * reduced, axis=0)
    reduced_cot = (scale_f * branch_cot_f).astype(jnp.bfloat16)
    narrow_sum = jnp.sum(reduced_cot.astype(jnp.float32), axis=0)
    reduce_sum = jnp.einsum("pf,pc->fc", active, reduced_cot, preferred_element_type=jnp.float32)
    active_cot = jnp.einsum(
        "pc,fc->pf", reduced_cot, reduce_weight, preferred_element_type=jnp.float32
    )
    (hidden_cot_f,) = gelu_pull(active_cot)
    hidden_cot = hidden_cot_f.astype(jnp.bfloat16)
    widen_sum = jnp.sum(hidden_cot.astype(jnp.float32), axis=0)
    expand_sum = jnp.einsum("pc,pf->cf", normed, hidden_cot, preferred_element_type=jnp.float32)
    normed_cot = jnp.einsum(
        "pf,cf->pc", hidden_cot, expand_weight, preferred_element_type=jnp.float32
    )
    filtered_cot, gain_sum, shift_sum = norm_pull(normed_cot)
    filtered_back = lax.all_to_all(
        filtered_cot.astype(jnp.bfloat16), "chan", split_axis=1, concat_axis=0, tiled=True
    )
    conv_cot = filtered_back.reshape(inputs.shape).astype(jnp.float32) * mask_f[..., None]
    offset_sum = jnp.sum(conv_cot, axis=(0, 1, 2))
    masked_cot, kernel_sum = conv_pull(conv_cot)
    input_gradient = cotangent.astype(jnp.float32) + masked_cot * mask_f[..., None]
    kernel_total, offset_total = lax.psum((kernel_sum, offset_sum), "batch")
    expand_total, widen_total, reduce_total, narrow_total, scale_total, gain_total, shift_total = (
        lax.psum(
            (expand_sum, widen_sum, reduce_sum, narrow_sum, scale_sum, gain_sum, shift_sum),
            ("batch", "chan"),
        )
    )
    return (
        block_output.astype(jnp.bfloat16),
        input_gradient.astype(jnp.bfloat16),
        kernel_total,
        offset_total,
        gain_total,
        shift_total,
        expand_total,
        widen_total,
        reduce_total,
        narrow_total,
        scale_total,
    )


def per_device(inputs, valid_mask, keep_mask, kernel, offset, norm_gain, norm_shift, expand_weight, expand_offset, reduce_weight,
               reduce_offset, layer_scale, cotangent):
    args = (inputs, valid_mask, keep_mask, kernel, offset, norm_gain, norm_shift, expand_weight, expand_offset, reduce_weight,
            reduce_offset, layer_scale, cotangent)
    images, side, _, channels = inputs.shape
    peers = expand_weight.shape[0] // channels
    if not (peers == 16 and channels % 8 == 0 and side == 24 and kernel.shape[0] == 7 and images <= L):
        return dense_form(*args)
    wide, perm, permt, plo, off, total = plan(valid_mask, keep_mask, side, SIZES[-1] * peers)
    most = lax.pmax(total, "batch")
    rest = (inputs, kernel, offset, norm_gain, norm_shift, expand_weight, expand_offset, reduce_weight, reduce_offset,
            layer_scale, cotangent, wide, perm, permt, plo, off)
    forms = [lambda ops, K=K, cid=cid: fast(K, cid, *ops[1]) for cid, K in enumerate(SIZES)]
    forms.append(lambda ops: dense_form(*ops[0]))
    which = sum((most > K * peers * L).astype(I32) for K in SIZES)
    return lax.switch(which, forms, (args, rest))


def solution(mesh):
    return jax.shard_map(
        per_device,
        mesh=mesh,
        in_specs=(
            P("batch", None, None, "chan"),
            P("batch", None, None),
            P("batch"),
            P(None, None, "chan"),
            P("chan"),
            P(),
            P(),
            P(),
            P(),
            P(),
            P(),
            P(),
            P("batch", None, None, "chan"),
        ),
        out_specs=(
            P("batch", None, None, "chan"),
            P("batch", None, None, "chan"),
            P(None, None, "chan"),
            P("chan"),
            P(),
            P(),
            P(),
            P(),
            P(),
            P(),
            P(),
        ),
        check_vma=False,
    )
```

```python
import functools

import jax
import jax.numpy as jnp
import numpy as np
from jax import lax
from jax.experimental import pallas as pl
from jax.experimental.pallas import tpu as pltpu
from jax.sharding import PartitionSpec as P

F32, BF16, I32 = jnp.float32, jnp.bfloat16, jnp.int32
MESH = pl.DeviceIdType.MESH
NT = (((1,), (1,)), ((), ()))
L = 128
ROOM, FULL = 15, 23
FACTOR = np.float32(1.0) / np.float32(0.9)
TAP = 21
SPAN = 384
BLOCK = 192


EDGE = 96
REACH = 9
MEGA = 1 << 20
QUARTERS = 4
AHEAD = 5
LAG = 0
ORDER = ("l", "h0", "H0", "h1", "s1", "w", "a", "r0", "H1", "h2", "r1", "H2", "h3", "c0", "H3", "h4", "c1", "H4", "g4", "c2", "G4", "g3",
         "c3", "G3", "g2", "k", "i", "G2", "g1", "G1", "g0", "K", "G0")


def pieces(slots, step):
    return [(k, min(step, slots - k)) for k in range(0, slots, step)]


def gelu_parts(h):
    a = 1.0 + np.float32(0.3275911 / np.sqrt(2.0)) * jnp.abs(h)
    t = pl.reciprocal(a, approx=True)
    t = t * (2.0 - a * t)
    e = jnp.exp(-0.5 * h * h)
    c = [0.5 * v for v in (0.254829592, -0.284496736, 1.421413741, -1.453152027, 1.061405429)]
    q = t * (c[0] + t * (c[1] + t * (c[2] + t * (c[3] + t * c[4])))) * e
    cdf = jnp.where(h >= 0, 1.0 - q, q)
    return h * cdf, cdf + (np.float32(1 / np.sqrt(2 * np.pi)) * h) * e


def plan_kernel(side, mask_ref, keep_ref, rows_ref, cols_ref, wide_ref, perm_ref, permt_ref, off_ref, plo_ref):
    N = keep_ref.shape[1]
    wide = jnp.sum(mask_ref[0], axis=0, keepdims=True)
    key = jnp.where(keep_ref[...] > 0, 1 + (wide >= 18).astype(I32) + (wide >= 24).astype(I32), 0).astype(F32)
    wide_ref[...] = wide
    key = jnp.concatenate([key, jnp.zeros((1, L - N), F32)], axis=1)
    a = lax.broadcasted_iota(I32, (L, L), 0)
    b = lax.broadcasted_iota(I32, (L, L), 1)
    eye = a == b
    here = jnp.broadcast_to(key, (L, L))
    there = jnp.broadcast_to(jnp.sum(jnp.where(eye, here, 0.0), axis=1, keepdims=True), (L, L))
    ahead = ((there > here) | ((there == here) & (a < b))).astype(F32)
    rank = jnp.sum(ahead, axis=0, keepdims=True)
    behind = ((here > there) | ((here == there) & (b < a))).astype(F32)
    rank_col = jnp.sum(behind, axis=1, keepdims=True)
    permt_ref[...] = ((rank == a.astype(F32)) & (here > 0.5)).astype(BF16)
    perm_ref[...] = ((rank_col == b.astype(F32)) & (there > 0.5)).astype(BF16)
    counts = [jnp.sum((key > t).astype(F32), axis=1, keepdims=True) for t in (2.5, 1.5, 0.5)]
    strides = [jnp.maximum(c, 16.0) for c in counts]
    off = sum(s * rows_ref[i:i + 1, :] for i, s in enumerate(strides)) + rows_ref[3:4, :]
    for i, c in enumerate(counts):
        off = off + c * rows_ref[4 + i:5 + i, :]
    off_ref[...] = off.astype(I32)
    ends = sum(s * cols_ref[:, i:i + 1] for i, s in enumerate(strides)) + cols_ref[:, 3:4]
    start = lax.broadcasted_iota(I32, (1, plo_ref.shape[1]), 1).astype(F32) * float(L)
    plo_ref[...] = jnp.sum((ends <= start).astype(F32), axis=0, keepdims=True).astype(I32)


def plan(valid_mask, keep_mask):
    N, side, _ = valid_mask.shape
    places = side * side
    reach = np.maximum(*np.meshgrid(np.arange(side), np.arange(side), indexing="ij")).reshape(-1)
    rings = [reach >= 18, (reach >= 14) & (reach < 18), reach < 14]
    before = np.stack([np.concatenate([[0], np.cumsum(m)]) for m in rings]).astype(np.float32)
    rows = np.zeros((8, 640), np.float32)
    rows[0:3, :places + 1] = before
    rows[3, places + 1:600] = MEGA
    for i in range(3):
        rows[4 + i, 600 + i] = 1.0
    cols = np.zeros((640, 8), np.float32)
    cols[:places, 0:3] = before[:, 1:].T
    cols[places:, 3] = MEGA
    vm = pl.BlockSpec(memory_space=pltpu.VMEM)
    wide, perm, permt, off, plo = pl.pallas_call(
        functools.partial(plan_kernel, side),
        grid=(1,),
        out_shape=[jax.ShapeDtypeStruct((1, N), I32), jax.ShapeDtypeStruct((L, L), BF16), jax.ShapeDtypeStruct((L, L), BF16),
                   jax.ShapeDtypeStruct((1, 640), I32), jax.ShapeDtypeStruct((1, 512), I32)],
        in_specs=[pl.BlockSpec((1, side, N), lambda i: (0, 0, 0)), vm, vm, vm],
        out_specs=[vm] * 5,
        name="plan",
    )(jnp.transpose(valid_mask, (1, 2, 0)), keep_mask[None, :], rows, cols)
    return wide, perm, permt, off, plo


def main_kernel(cfg, plo, off, x_hbm, s_ref, cot_hbm, perm_ref, permt_ref, kern_ref, bias_ref, band_ref, w1_hbm, w2_hbm,
                gain_ref, shift_ref, b2_ref, scale_ref, wide_bias_ref,
                br_out, ig_out, rg_out, eg_out, small_out, kg_out, og_out,
                x_ref, cot_ref, w1_ref, w2_ref, w1t_ref, w2t_ref,
                xf, srt, xpad, cpad, tall, vecs, taps, flip, cols, b1_ref, bc_send, f_send, bc_recv, f_recv, fc_recv,
                rg_acc, eg_acc, vec_acc, wid_acc, res, hold, small, small_recv, kg_acc, og_acc, kg_recv, og_recv,
                ld_sem, in_ssem, in_rsem, out_ssem, out_rsem, st_sem, ex_ssem, ex_rsem, sm_ssem, sm_rsem, kg_ssem, kg_rsem):
    side, C, N, K, NC, step = cfg
    C2 = NC * C
    FF = w2_ref.shape[0]
    rows = side * C
    maps = side * side
    b = lax.axis_index("batch")
    me = lax.axis_index("chan")
    parts = pieces(K, step)

    cot_loads = [pltpu.make_async_copy(cot_hbm.at[pl.ds(j * side // QUARTERS, side // QUARTERS)],
                                       cot_ref.at[pl.ds(j * side // QUARTERS, side // QUARTERS)], ld_sem.at[j]) for j in range(QUARTERS)]
    x_loads = [pltpu.make_async_copy(x_hbm.at[pl.ds(j * side // QUARTERS, side // QUARTERS)],
                                     x_ref.at[pl.ds(j * side // QUARTERS, side // QUARTERS)], ld_sem.at[QUARTERS + j]) for j in range(QUARTERS)]
    w_loads = [pltpu.make_async_copy(s, d, ld_sem.at[2 * QUARTERS + i]) for i, (s, d) in enumerate(((w1_hbm, w1_ref), (w2_hbm, w2_ref)))]
    for cp in cot_loads:
        cp.start()

    bar = pltpu.get_barrier_semaphore()
    def greet(m, _):
        pl.semaphore_signal(bar, inc=1, device_id=(b, lax.rem(me + m, NC)), device_id_type=MESH)
        return 0
    lax.fori_loop(1, NC, greet, 0)
    pl.semaphore_signal(bar, inc=1, device_id=(1 - b, me), device_id_type=MESH)

    lane = lax.broadcasted_iota(I32, (C, L), 1)
    perm = perm_ref[...]
    permt = permt_ref[...]
    s = s_ref[...]

    def send(src, dst, s0, n, ssem, rsem):
        sl = pl.ds(s0, n)
        def one(m, _):
            t = lax.rem(me + m, NC)
            pltpu.make_async_remote_copy(
                src_ref=src.at[sl, t], dst_ref=dst.at[sl, me], send_sem=ssem, recv_sem=rsem,
                device_id=(b, t), device_id_type=MESH).start()
            return 0
        lax.fori_loop(1, NC, one, 0)
        pltpu.make_async_copy(src.at[sl, me], dst.at[sl, me], rsem).start()

    def arrived(dst, s0, n, rsem):
        ref = dst.at[pl.ds(s0, n)]
        pltpu.make_async_copy(ref, ref, rsem).wait()

    def sent(src, ssem):
        ref = src.at[:, pl.ds(0, NC - 1)]
        pltpu.make_async_copy(ref, ref, ssem).wait()

    def pack(dst, s0, n):
        def group(g):
            p0 = plo[0, g]
            acc = jnp.zeros((C, L), F32)
            for t in range(REACH):
                sh = off[0, p0 + t] - g * L
                v = srt[p0 + t]
                acc = jnp.where(lane >= sh, pltpu.roll(v, lax.bitwise_and(sh, L - 1), 1), acc)
            return acc
        B = 8
        def body(h, _):
            sl = s0 + h * B // NC
            d0 = lax.rem(h * B, NC)
            accs = [group(sl * NC + d0 + i) for i in range(B)]
            for i in range(B):
                dst[sl, d0 + i] = accs[i].astype(BF16)
            return 0
        lax.fori_loop(0, n * NC // B, body, 0, unroll=2)

    def unpack(src, i, j):
        p = i * side + j
        o = off[0, p]
        g = lax.shift_right_logical(o, 7)
        r = lax.bitwise_and(o, L - 1)
        g2 = jnp.minimum(g + 1, K * NC - 1)
        a = src[lax.shift_right_logical(g, 4), lax.bitwise_and(g, NC - 1)].astype(F32)
        v = src[lax.shift_right_logical(g2, 4), lax.bitwise_and(g2, NC - 1)].astype(F32)
        v = jnp.where(lane >= r, a, v)
        v = pltpu.roll(v, lax.bitwise_and(L - r, L - 1), 1)
        m = jnp.maximum(i, j)
        n = jnp.where(m < 14, off[0, 602], jnp.where(m < 18, off[0, 601], off[0, 600]))
        return jnp.where(lane < n, v, 0.0)

    srt[maps] = jnp.zeros((C, L), F32)
    def bc_row(i, _):
        vals = []
        for j in range(side):
            m = jnp.where(s > jnp.maximum(i, j), FACTOR, F32(0.0))
            vals.append(cot_ref[i, j].astype(F32) * m)
        v = jnp.concatenate(vals, axis=0).astype(BF16)
        srt[pl.ds(i * side, side)] = jnp.dot(v, perm_ref[0:N, :], preferred_element_type=F32).reshape(side, C, L)
        return 0
    for j, cp in enumerate(cot_loads):
        cp.wait()
        lax.fori_loop(j * side // QUARTERS, (j + 1) * side // QUARTERS, bc_row, 0)
    for cp in x_loads:
        cp.start()
    pl.semaphore_wait(bar, NC)
    for k, (s0, n) in enumerate(parts):
        pack(bc_send, s0, n)
        send(bc_send, bc_recv, s0, n, in_ssem.at[0], in_rsem.at[0, k])

    for cp in w_loads:
        cp.start()
    tall[...] = jnp.zeros_like(tall)
    ks = kern_ref.shape[0]
    for a in range(ks):
        row = kern_ref[a].astype(F32)
        at = TAP + a * side
        tall[0, at:at + ks, 0:C] = row
        at = TAP + (ks - 1 - a) * side
        for i in range(ks):
            tall[1, at + ks - 1 - i:at + ks - i, 0:C] = row[i:i + 1, :]
    taps[...] = jnp.transpose(tall[0])[0:C, :]
    flip[...] = jnp.transpose(tall[1])[0:C, :]
    def x_row(i, _):
        for j in range(side):
            m = (s > jnp.maximum(i, j)).astype(F32)
            xf[pl.ds(pl.multiple_of(i * rows + j * C, 8), C), 0:N] = x_ref[i, j].astype(F32) * m
        return 0
    xpad[...] = jnp.zeros_like(xpad)
    for j, cp in enumerate(x_loads):
        cp.wait()
        lax.fori_loop(j * side // QUARTERS, (j + 1) * side // QUARTERS, x_row, 0)

    def banded(tap, win):
        tap = jnp.broadcast_to(tap, (8, SPAN))
        tiles = [pltpu.roll(tap, 8 * k, 1, stride=1, stride_axis=0) * band_ref[8 * k:8 * k + 8, :] for k in range(BLOCK // 8)]
        return jnp.dot(jnp.concatenate(tiles, axis=0).astype(BF16), win, preferred_element_type=F32)

    def windows(pad, c):
        return jnp.concatenate([pad[c, BLOCK * g:BLOCK * g + SPAN, :] for g in range(maps // BLOCK)], axis=1)

    def spread(c, out):
        for g in range(maps // BLOCK):
            xf[pl.ds(g * BLOCK * C + c, BLOCK, stride=C), :] = out[:, g * L:(g + 1) * L]

    def channel(c, _):
        xpad[c, EDGE:EDGE + maps, 0:N] = xf[pl.ds(c, maps, stride=C), :][:, 0:N].astype(BF16)
        spread(c, banded(taps[pl.ds(c, 1), :], windows(xpad, c)))
        return 0
    lax.fori_loop(0, C, channel, 0)

    vecs[...] = jnp.zeros_like(vecs)
    vecs[8:9, 0:C] = bias_ref[...].astype(F32).reshape(1, C)
    for i, ref in enumerate((gain_ref, shift_ref, b2_ref, scale_ref)):
        vecs[i:i + 1, :] = ref[...].astype(F32).reshape(1, C2)
    for i in range(FF // C2):
        vecs[4 + i:5 + i, :] = wide_bias_ref[i * C2:(i + 1) * C2].astype(F32).reshape(1, C2)
    turned = jnp.transpose(vecs[...])
    bias = jnp.concatenate([jnp.broadcast_to(turned[0:C, 8:9], (C, L))] * side, axis=0)
    def f_row(i, _):
        v = (xf[pl.ds(pl.multiple_of(i * rows, 8), rows), :] + bias).astype(BF16)
        srt[pl.ds(i * side, side)] = jnp.dot(v, perm, preferred_element_type=F32).reshape(side, C, L)
        return 0
    lax.fori_loop(0, side, f_row, 0)
    for k, (s0, n) in enumerate(parts):
        pack(f_send, s0, n)
        if k < AHEAD:
            send(f_send, f_recv, s0, n, in_ssem.at[1], in_rsem.at[1, k])

    for cp in w_loads:
        cp.wait()
    w1t_ref[...] = jnp.transpose(w1_ref[...])
    w2t_ref[...] = jnp.transpose(w2_ref[...])
    cols[...] = turned
    for i in range(FF // C2):
        b1_ref[i * C2:(i + 1) * C2, :] = turned[:, 4 + i:5 + i]
    rg_acc[...] = jnp.zeros_like(rg_acc)
    eg_acc[...] = jnp.zeros_like(eg_acc)
    vec_acc[...] = jnp.zeros_like(vec_acc)
    wid_acc[...] = jnp.zeros_like(wid_acc)
    FB = 256
    whole = K // step


    def feed(k):
        if isinstance(k, int):
            if k + AHEAD < len(parts):
                s0, n = parts[k + AHEAD]
                send(f_send, f_recv, s0, n, in_ssem.at[1], in_rsem.at[1, k + AHEAD])
            return
        @pl.when(k + AHEAD < whole)
        def _():
            send(f_send, f_recv, (k + AHEAD) * step, step, in_ssem.at[1], in_rsem.at[1, k + AHEAD])
        for j in range(whole, len(parts)):
            @pl.when(k + AHEAD == j)
            def _():
                send(f_send, f_recv, parts[j][0], parts[j][1], in_ssem.at[1], in_rsem.at[1, j])

    def mlp(s0, n, k):
        W = n * L

        def fold(v):
            out = v[:, 0:L]
            for t in range(1, n):
                out = out + v[:, t * L:(t + 1) * L]
            return out

        def load(ref):
            return jnp.concatenate([ref[s0 + t].astype(F32).reshape(C2, L) for t in range(n)], axis=1)

        def store(ref, v):
            for t in range(n):
                ref[s0 + t] = v[:, t * L:(t + 1) * L].reshape(NC, C, L).astype(BF16)

        arrived(bc_recv, s0, n, in_rsem.at[0, k])
        arrived(f_recv, s0, n, in_rsem.at[1, k])
        feed(k)
        gain, shift, b2, scale = (cols[:, i:i + 1] for i in range(4))
        f = load(f_recv)
        d = f - jnp.mean(f, axis=0, keepdims=True)
        inv = lax.rsqrt(jnp.mean(d * d, axis=0, keepdims=True) + 1e-6)
        xhat = d * inv
        normed = (xhat * gain + shift).astype(BF16)
        bc = load(bc_recv)
        rc = (scale * bc).astype(BF16)
        vec_acc[2] += fold(rc.astype(F32))
        red = jnp.zeros((C2, W), F32)
        nc = jnp.zeros((C2, W), F32)
        for fb in range(FF // FB):
            r = slice(fb * FB, (fb + 1) * FB)
            h = jnp.dot(w1t_ref[r, :], normed, preferred_element_type=F32) + b1_ref[r, :]
            act, slope = gelu_parts(h)
            act = act.astype(BF16)
            ac = jnp.dot(w2_ref[r, :], rc, preferred_element_type=F32)
            hc = (ac * slope).astype(BF16)
            red = red + jnp.dot(w2t_ref[:, r], act, preferred_element_type=F32)
            nc = nc + jnp.dot(w1_ref[:, r], hc, preferred_element_type=F32)
            rg_acc[r, :] += lax.dot_general(act, rc, NT, preferred_element_type=F32)
            eg_acc[r, :] += lax.dot_general(hc, normed, NT, preferred_element_type=F32)
            wid_acc[r, :] += fold(hc.astype(F32))
        red = red + b2
        store(bc_recv, scale * red)
        vec_acc[3] += fold(bc * red)
        vec_acc[0] += fold(nc * xhat)
        vec_acc[1] += fold(nc)
        q = nc * gain
        m1 = jnp.mean(q, axis=0, keepdims=True)
        m2 = jnp.mean(q * xhat, axis=0, keepdims=True)
        store(f_recv, inv * (q - m1 - xhat * m2))

    def mlp_step(k, _):
        mlp(k * step, step, k)
        @pl.when(k >= LAG)
        def _():
            j = k - LAG
            send(f_recv, fc_recv, j * step, step, out_ssem.at[0], out_rsem.at[0, j])
        return 0
    lax.fori_loop(0, whole, mlp_step, 0)
    for k, (s0, n) in list(enumerate(parts))[whole:]:
        mlp(s0, n, k)


    ones = jnp.ones((8, L), F32)
    def row_of(v):
        return lax.dot_general(ones, v, NT, precision=lax.Precision.HIGHEST, preferred_element_type=F32)
    sub = lax.broadcasted_iota(I32, (8, C2), 0)
    tot = jnp.zeros((8, C2), F32)
    for i in range(4):
        tot = tot + jnp.where(sub == i, row_of(vec_acc[i]), 0.0)
    for i in range(FF // C2):
        tot = tot + jnp.where(sub == 4 + i, row_of(wid_acc[i * C2:(i + 1) * C2, :]), 0.0)
    over = jnp.where(off[0, maps] > K * NC * L, F32(1.0), F32(0.0))
    small[0:8, :] = tot
    small[8:16, :] = jnp.zeros((8, C2), F32) + over

    accs, outs = (rg_acc, eg_acc), (rg_out, eg_out)
    def peer(bit):
        if bit < 0:
            return (1 - b, me), b
        w = 1 << bit
        on = lax.rem(me // w, 2)
        return (b, me + w - 2 * w * on), on
    orders = ((-1, -1), (0, 1), (1, 0), (2, 2), (3, 3))
    base = [0, 0]
    legs = []
    lo, span = 0, FF
    for st, bits in enumerate(orders):
        span //= 2
        leg = []
        for a in range(2):
            dev, on = peer(bits[a])
            theirs = pl.multiple_of(base[a] + (1 - on) * span, 16)
            base[a] = pl.multiple_of(base[a] + on * span, 16)
            cp = pltpu.make_async_remote_copy(
                src_ref=hold.at[a, pl.ds(0, span)], dst_ref=res.at[a, pl.ds(lo, span)],
                send_sem=ex_ssem.at[a, st], recv_sem=ex_rsem.at[a, st], device_id=dev, device_id_type=MESH)
            leg.append((cp, theirs, base[a], dev))
        dev, _ = peer(bits[0])
        sc = pltpu.make_async_remote_copy(
            src_ref=small, dst_ref=small_recv.at[st], send_sem=sm_ssem.at[st], recv_sem=sm_rsem.at[st],
            device_id=dev, device_id_type=MESH)
        legs.append((lo, span, leg, sc))
        lo += span

    def halve_start(st):
        lo, span, leg, sc = legs[st]
        for a in range(2):
            cp, theirs, _, _ = leg[a]
            hold[a, 0:span, :] = accs[a][pl.ds(theirs, span), :].astype(BF16)
            cp.start()
        sc.start()

    def halve_end(st):
        lo, span, leg, sc = legs[st]
        for a in range(2):
            cp, _, mine, _ = leg[a]
            cp.wait()
            accs[a][pl.ds(mine, span), :] += res[a, lo:lo + span, :].astype(F32)
        sc.wait()
        small[...] += small_recv[st]

    back = {}
    def gather_start(st):
        lo, span, leg, _ = legs[st]
        back[st] = []
        for a in range(2):
            ref = outs[a].at[pl.ds(leg[a][2], span)]
            cp = pltpu.make_async_remote_copy(
                src_ref=ref, dst_ref=ref, send_sem=ex_ssem.at[a, 5 + st], recv_sem=ex_rsem.at[a, 5 + st],
                device_id=leg[a][3], device_id_type=MESH)
            cp.start()
            back[st].append(cp)

    def gather_end(st):
        for cp in back[st]:
            cp.wait()

    def bulk(kind, k):
        s0, n = parts[k]
        src, dst = ((f_recv, fc_recv), (bc_recv, br_out))[kind]
        send(src, dst, s0, n, out_ssem.at[kind], out_rsem.at[kind, k])

    late = [(0, k) for k in range(max(whole - LAG, 0), len(parts))]
    todo = late + [(1, k) for k in range(len(parts))]
    def some(share):
        for _ in range(min(share, len(todo))):
            bulk(*todo.pop(0))

    def fc_row(i, _):
        vals = [unpack(fc_recv, i, j) for j in range(side)]
        tot = vals[0]
        for v in vals[1:]:
            tot = tot + v
        og_acc[...] += tot
        v = jnp.concatenate(vals, axis=0).astype(BF16)
        xf[pl.ds(pl.multiple_of(i * rows, 8), rows), :] = jnp.dot(v, permt, preferred_element_type=F32)
        return 0

    def channel_back(c, _):
        cpad[c, EDGE:EDGE + maps, :] = xf[pl.ds(c, maps, stride=C), :].astype(BF16)
        spread(c, banded(flip[pl.ds(c, 1), :], windows(cpad, c)))
        mid = jnp.concatenate([cpad[c, EDGE + BLOCK * g:EDGE + BLOCK * (g + 1), :] for g in range(maps // BLOCK)], axis=1)
        gram = lax.dot_general(mid, windows(xpad, c), NT, preferred_element_type=F32) * band_ref[...]
        acc = jnp.zeros((8, SPAN), F32)
        for k in range(BLOCK // 8):
            acc = acc + pltpu.roll(gram[8 * k:8 * k + 8, :], (SPAN - 8 * k) % SPAN, 1)
        kg_acc[c] = acc
        return 0

    swap = [pltpu.make_async_remote_copy(src_ref=v, dst_ref=r, send_sem=kg_ssem.at[i], recv_sem=kg_rsem.at[i],
                                         device_id=(1 - b, me), device_id_type=MESH)
            for i, (v, r) in enumerate(((kg_acc, kg_recv), (og_acc, og_recv)))]

    def ig_row(i, _):
        for j in range(side):
            m = (s > jnp.maximum(i, j)).astype(F32)
            v = xf[pl.ds(pl.multiple_of(i * rows + j * C, 8), C), :][:, 0:N]
            x_ref[i, j] = (cot_ref[i, j].astype(F32) + v * m).astype(BF16)
        return 0

    put = pltpu.make_async_copy(x_ref, ig_out, st_sem)

    def share(n, of, body, total):
        lax.fori_loop(n * total // of, (n + 1) * total // of, body, 0)

    cpad[...] = jnp.zeros_like(cpad)
    og_acc[...] = jnp.zeros_like(og_acc)
    for word in ORDER:
        op, num = word[0], int(word[1:] or 0)
        if op == "h":
            halve_start(num)
        elif op == "H":
            halve_end(num)
            if num == 4:
                small_out[...] = small[...]
                for a in range(2):
                    mine = legs[4][2][a][2]
                    outs[a][pl.ds(mine, legs[4][1]), :] = accs[a][pl.ds(mine, legs[4][1]), :].astype(BF16)
        elif op == "g":
            gather_start(num)
        elif op == "G":
            gather_end(num)
        elif op == "s":
            some(num)
        elif op == "a":
            some(len(todo))
        elif op == "l":
            while todo[0][0] == 0:
                some(1)
        elif op == "w":
            for k, (s0, n) in enumerate(parts):
                arrived(fc_recv, s0, n, out_rsem.at[0, k])
        elif op == "r":
            share(num, 2, fc_row, side)
        elif op == "c":
            share(num, 4, channel_back, C)
        elif op == "k":
            for cp in swap:
                cp.start()
        elif op == "K":
            for cp in swap:
                cp.wait()
            kg_out[...] = kg_acc[...] + kg_recv[...]
            og_out[...] = og_acc[...] + og_recv[...]
        elif op == "i":
            share(0, 1, ig_row, side)
            put.start()

    put.wait()
    for k, (s0, n) in enumerate(parts):
        arrived(br_out, s0, n, out_rsem.at[1, k])
    sent(bc_send, in_ssem.at[0])
    sent(f_send, in_ssem.at[1])
    sent(f_recv, out_ssem.at[0])
    sent(bc_recv, out_ssem.at[1])


def tail_kernel(cfg, off, x_hbm, permt_ref, br_hbm, ig_hbm, rg_hbm, eg_hbm, small_ref, kg_ref, og_ref,
                out_hbm, ig_out, rg_out, eg_out, kg_out, og_out, wide_out, over_out, *rest):
    side, C, N, K, NC, _ = cfg
    vec_outs = rest[:4]
    x_ref, br_ref, ig_ref, rg_ref, eg_ref, rg_f, eg_f, sem = rest[4:]
    lane = lax.broadcasted_iota(I32, (C, L), 1)
    ks = kg_out.shape[0]
    C2 = small_ref.shape[1]
    br_in = pltpu.make_async_copy(br_hbm, br_ref, sem.at[0])
    rg_in = pltpu.make_async_copy(rg_hbm, rg_ref, sem.at[1])
    eg_in = pltpu.make_async_copy(eg_hbm, eg_ref, sem.at[2])
    ig_in = pltpu.make_async_copy(ig_hbm, ig_ref, sem.at[3])
    x_in = [pltpu.make_async_copy(x_hbm.at[pl.ds(j * side // QUARTERS, side // QUARTERS)],
                                  x_ref.at[pl.ds(j * side // QUARTERS, side // QUARTERS)], sem.at[8 + j]) for j in range(QUARTERS)]
    br_in.start()
    for cp in x_in:
        cp.start()
    rg_in.start()
    eg_in.start()
    ig_in.start()
    permt = permt_ref[...]

    def unpack(i, j):
        o = off[0, i * side + j]
        g = lax.shift_right_logical(o, 7)
        r = lax.bitwise_and(o, L - 1)
        v = jnp.where(lane >= r, br_ref[g].astype(F32), br_ref[jnp.minimum(g + 1, K * NC - 1)].astype(F32))
        v = pltpu.roll(v, lax.bitwise_and(L - r, L - 1), 1)
        m = jnp.maximum(i, j)
        n = jnp.where(m < 14, off[0, 602], jnp.where(m < 18, off[0, 601], off[0, 600]))
        return jnp.where(lane < n, v, 0.0)

    def br_row(i, _):
        v = jnp.concatenate([unpack(i, j) for j in range(side)], axis=0).astype(BF16)
        v = jnp.dot(v, permt, preferred_element_type=F32)
        for j in range(side):
            x_ref[i, j] = (x_ref[i, j].astype(F32) + FACTOR * v[j * C:(j + 1) * C, 0:N]).astype(BF16)
        return 0

    br_in.wait()
    x_out = []
    for j, cp in enumerate(x_in):
        cp.wait()
        sl = pl.ds(j * side // QUARTERS, side // QUARTERS)
        lax.fori_loop(j * side // QUARTERS, (j + 1) * side // QUARTERS, br_row, 0, unroll=2)
        put = pltpu.make_async_copy(x_ref.at[sl], out_hbm.at[sl], sem.at[12 + j])
        put.start()
        x_out.append(put)
        if j == 0:
            ig_in.wait()
            put = pltpu.make_async_copy(ig_ref, ig_out, sem.at[4])
            put.start()
            x_out.append(put)
        if j == 1:
            rg_in.wait()
            rg_f[...] = rg_ref[...].astype(F32)
            put = pltpu.make_async_copy(rg_f, rg_out, sem.at[5])
            put.start()
            x_out.append(put)
        if j == 2:
            eg_in.wait()
            eg_f[...] = jnp.transpose(eg_ref[...].astype(F32))
            put = pltpu.make_async_copy(eg_f, eg_out, sem.at[6])
            put.start()
            x_out.append(put)

    total = kg_ref[:, 0, :]
    for q in range(1, 8):
        total = total + pltpu.roll(kg_ref[:, q, :], SPAN - q, 1)
    turned = jnp.transpose(total)
    for a in range(ks):
        kg_out[a] = turned[TAP + a * side:TAP + a * side + ks, :]
    og_out[...] = jnp.sum(jnp.transpose(og_ref[...]), axis=0)
    for i, ref in enumerate(vec_outs):
        ref[...] = small_ref[i, :]
    for i in range(wide_out.shape[0] // C2):
        wide_out[i * C2:(i + 1) * C2] = small_ref[4 + i, :]
    over_out[...] = small_ref[8, 0:L]
    for put in x_out:
        put.wait()


def packed_form(K, step, cid, inputs, kernel, offset, norm_gain, norm_shift, expand_weight, expand_offset, reduce_weight, reduce_offset,
                layer_scale, cotangent, wide, perm, permt, off, plo):
    N, side, _, C = inputs.shape
    C2, FF = expand_weight.shape
    NC = C2 // C
    cfg = (side, C, N, K, NC, step)
    ks = kernel.shape[0]
    x = jnp.transpose(inputs, (1, 2, 3, 0))
    cot = jnp.transpose(cotangent, (1, 2, 3, 0))
    r = np.arange(BLOCK)
    l = np.arange(SPAN)
    band = (np.abs(l[None] % side - r[:, None] % side) <= ks // 2).astype(np.float32)
    vm = pl.BlockSpec(memory_space=pltpu.VMEM)
    sm = pl.BlockSpec(memory_space=pltpu.SMEM)
    hbm = pl.BlockSpec(memory_space=pl.ANY)
    blk = (K, NC, C, L)
    img = (side, side, C, N)
    steps = len(pieces(K, step))
    held = FF - FF // 32
    sd = jax.ShapeDtypeStruct
    dma = pltpu.SemaphoreType.DMA
    br, ig, rg, eg, small, kg, og = pl.pallas_call(
        functools.partial(main_kernel, cfg),
        out_shape=[sd(blk, BF16), sd(img, BF16), sd((FF, C2), BF16), sd((FF, C2), BF16), sd((16, C2), F32),
                   sd((C, 8, SPAN), F32), sd((C, L), F32)],
        in_specs=[sm, sm, hbm, vm, hbm, vm, vm, vm, vm, vm, hbm, hbm] + [vm] * 5,
        out_specs=[hbm, hbm, vm, vm, vm, vm, vm],
        scratch_shapes=[
            pltpu.VMEM(img, BF16), pltpu.VMEM(img, BF16),
            pltpu.VMEM((C2, FF), BF16), pltpu.VMEM((FF, C2), BF16), pltpu.VMEM((FF, C2), BF16), pltpu.VMEM((C2, FF), BF16),
            pltpu.VMEM((side * side * C, L), F32), pltpu.VMEM((586, C, L), F32),
            pltpu.VMEM((C, 768, L), BF16), pltpu.VMEM((C, 768, L), BF16),
            pltpu.VMEM((2, SPAN, L), F32), pltpu.VMEM((16, C2), F32),
            pltpu.VMEM((C, SPAN), F32), pltpu.VMEM((C, SPAN), F32), pltpu.VMEM((C2, 16), F32), pltpu.VMEM((FF, 1), F32),
            pltpu.VMEM(blk, BF16), pltpu.VMEM(blk, BF16), pltpu.VMEM(blk, BF16), pltpu.VMEM(blk, BF16), pltpu.VMEM(blk, BF16),
            pltpu.VMEM((FF, C2), F32), pltpu.VMEM((FF, C2), F32), pltpu.VMEM((4, C2, L), F32), pltpu.VMEM((FF, L), F32),
            pltpu.VMEM((2, held, C2), BF16), pltpu.VMEM((2, FF // 2, C2), BF16),
            pltpu.VMEM((16, C2), F32), pltpu.VMEM((5, 16, C2), F32),
            pltpu.VMEM((C, 8, SPAN), F32), pltpu.VMEM((C, L), F32), pltpu.VMEM((C, 8, SPAN), F32), pltpu.VMEM((C, L), F32),
            dma((2 * QUARTERS + 2,)), dma((2,)), dma((2, steps)), dma((2,)), dma((2, steps)), dma,
            dma((2, 10)), dma((2, 10)), dma((5,)), dma((5,)), dma((2,)), dma((2,)),
        ],
        compiler_params=pltpu.CompilerParams(collective_id=cid, has_side_effects=True, vmem_limit_bytes=63 << 20),
        name="main_%d" % K,
    )(plo, off, x, wide, cot, perm, permt, kernel, offset, band, expand_weight, reduce_weight,
      norm_gain, norm_shift, reduce_offset, layer_scale, expand_offset)
    row = sd((C2,), F32)
    out, ig, rg, eg, kg, og, widen, over, gain, shift, narrow, scale = pl.pallas_call(
        functools.partial(tail_kernel, cfg),
        out_shape=[sd(img, BF16), sd(img, BF16), sd((FF, C2), F32), sd((C2, FF), F32), sd((ks, ks, C), F32), sd((C,), F32),
                   sd((FF,), F32), sd((L,), F32), row, row, row, row],
        in_specs=[sm, hbm, vm, hbm, hbm, hbm, hbm, vm, vm, vm],
        out_specs=[hbm] * 4 + [vm] * 8,
        scratch_shapes=[pltpu.VMEM(img, BF16), pltpu.VMEM((K * NC, C, L), BF16), pltpu.VMEM(img, BF16), pltpu.VMEM((FF, C2), BF16),
                        pltpu.VMEM((FF, C2), BF16), pltpu.VMEM((FF, C2), F32), pltpu.VMEM((C2, FF), F32), dma((16,))],
        compiler_params=pltpu.CompilerParams(vmem_limit_bytes=60 << 20),
        name="tail_%d" % K,
    )(off, x, permt, br.reshape(K * NC, C, L), ig, rg, eg, small, kg, og)
    return (jnp.transpose(out, (3, 0, 1, 2)), jnp.transpose(ig, (3, 0, 1, 2)), kg, og, gain, shift, eg, widen, rg, narrow, scale), over


keep_rate = 0.9
epsilon = 1e-06


def exact_gelu(values):
    return jax.nn.gelu(values, approximate=False)


def layer_norm(values, gain, shift):
    center = jnp.mean(values, axis=-1, keepdims=True)
    spread = jnp.mean(jnp.square(values - center), axis=-1, keepdims=True)
    return (values - center) * lax.rsqrt(spread + epsilon) * gain + shift


def dense_form(
    inputs,
    valid_mask,
    keep_mask,
    kernel,
    offset,
    norm_gain,
    norm_shift,
    expand_weight,
    expand_offset,
    reduce_weight,
    reduce_offset,
    layer_scale,
    cotangent,
):
    images, height, breadth, channels = inputs.shape
    kside = kernel.shape[0]
    pixels = images * height * breadth
    mask_f = valid_mask.astype(jnp.float32)
    factor = mask_f * (keep_mask.astype(jnp.float32) / keep_rate)[:, None, None]

    def local_conv(source, kern):
        return lax.conv_general_dilated(
            source,
            kern.reshape(kside, kside, 1, channels),
            (1, 1),
            "SAME",
            dimension_numbers=("NHWC", "HWIO", "NHWC"),
            feature_group_count=channels,
            precision=lax.Precision.HIGHEST,
        )

    masked = inputs.astype(jnp.float32) * mask_f[..., None]
    conv_out, conv_pull = jax.vjp(local_conv, masked, kernel.astype(jnp.float32))
    filtered = ((conv_out + offset.astype(jnp.float32)) * mask_f[..., None]).astype(jnp.bfloat16)
    flat_filtered = filtered.reshape(pixels, channels)
    pixel_rows = lax.all_to_all(flat_filtered, "chan", split_axis=0, concat_axis=1, tiled=True)
    normed_f, norm_pull = jax.vjp(
        layer_norm,
        pixel_rows.astype(jnp.float32),
        norm_gain.astype(jnp.float32),
        norm_shift.astype(jnp.float32),
    )
    normed = normed_f.astype(jnp.bfloat16)
    hidden = jnp.dot(
        normed, expand_weight, preferred_element_type=jnp.float32
    ) + expand_offset.astype(jnp.float32)
    active_f, gelu_pull = jax.vjp(exact_gelu, hidden)
    active = active_f.astype(jnp.bfloat16)
    reduced = jnp.dot(
        active, reduce_weight, preferred_element_type=jnp.float32
    ) + reduce_offset.astype(jnp.float32)
    scale_f = layer_scale.astype(jnp.float32)
    branch = (scale_f * reduced).astype(jnp.bfloat16)
    branch_back = lax.all_to_all(branch, "chan", split_axis=1, concat_axis=0, tiled=True)
    block_output = inputs.astype(jnp.float32) + factor[..., None] * branch_back.reshape(
        inputs.shape
    ).astype(jnp.float32)
    local_cot = (
        (cotangent.astype(jnp.float32) * factor[..., None])
        .astype(jnp.bfloat16)
        .reshape(pixels, channels)
    )
    branch_cot = lax.all_to_all(local_cot, "chan", split_axis=0, concat_axis=1, tiled=True)
    branch_cot_f = branch_cot.astype(jnp.float32)
    scale_sum = jnp.sum(branch_cot_f * reduced, axis=0)
    reduced_cot = (scale_f * branch_cot_f).astype(jnp.bfloat16)
    narrow_sum = jnp.sum(reduced_cot.astype(jnp.float32), axis=0)
    reduce_sum = jnp.einsum("pf,pc->fc", active, reduced_cot, preferred_element_type=jnp.float32)
    active_cot = jnp.einsum(
        "pc,fc->pf", reduced_cot, reduce_weight, preferred_element_type=jnp.float32
    )
    (hidden_cot_f,) = gelu_pull(active_cot)
    hidden_cot = hidden_cot_f.astype(jnp.bfloat16)
    widen_sum = jnp.sum(hidden_cot.astype(jnp.float32), axis=0)
    expand_sum = jnp.einsum("pc,pf->cf", normed, hidden_cot, preferred_element_type=jnp.float32)
    normed_cot = jnp.einsum(
        "pf,cf->pc", hidden_cot, expand_weight, preferred_element_type=jnp.float32
    )
    filtered_cot, gain_sum, shift_sum = norm_pull(normed_cot)
    filtered_back = lax.all_to_all(
        filtered_cot.astype(jnp.bfloat16), "chan", split_axis=1, concat_axis=0, tiled=True
    )
    conv_cot = filtered_back.reshape(inputs.shape).astype(jnp.float32) * mask_f[..., None]
    offset_sum = jnp.sum(conv_cot, axis=(0, 1, 2))
    masked_cot, kernel_sum = conv_pull(conv_cot)
    input_gradient = cotangent.astype(jnp.float32) + masked_cot * mask_f[..., None]
    kernel_total, offset_total = lax.psum((kernel_sum, offset_sum), "batch")
    expand_total, widen_total, reduce_total, narrow_total, scale_total, gain_total, shift_total = (
        lax.psum(
            (expand_sum, widen_sum, reduce_sum, narrow_sum, scale_sum, gain_sum, shift_sum),
            ("batch", "chan"),
        )
    )
    return (
        block_output.astype(jnp.bfloat16),
        input_gradient.astype(jnp.bfloat16),
        kernel_total,
        offset_total,
        gain_total,
        shift_total,
        expand_total,
        widen_total,
        reduce_total,
        narrow_total,
        scale_total,
    )


def per_device(inputs, valid_mask, keep_mask, kernel, offset, norm_gain, norm_shift, expand_weight, expand_offset, reduce_weight,
               reduce_offset, layer_scale, cotangent):
    images, side, _, channels = inputs.shape
    peers = expand_weight.shape[0] // channels
    if not (peers == 16 and channels % 8 == 0 and side == 24 and kernel.shape[0] == 7 and images <= L):
        return dense_form(inputs, valid_mask, keep_mask, kernel, offset, norm_gain, norm_shift, expand_weight, expand_offset,
                          reduce_weight, reduce_offset, layer_scale, cotangent)
    args = (inputs, kernel, offset, norm_gain, norm_shift, expand_weight, expand_offset, reduce_weight, reduce_offset, layer_scale,
            cotangent) + tuple(plan(valid_mask, keep_mask))
    outs, over = packed_form(ROOM, 2, 1, *args)
    again = lambda state: (packed_form(FULL, 1, 2, *args)[0], jnp.zeros((L,), F32))
    return lax.while_loop(lambda state: state[1][0] > 0.5, again, (outs, over))[0]


def solution(mesh):
    return jax.shard_map(
        per_device,
        mesh=mesh,
        in_specs=(
            P("batch", None, None, "chan"),
            P("batch", None, None),
            P("batch"),
            P(None, None, "chan"),
            P("chan"),
            P(),
            P(),
            P(),
            P(),
            P(),
            P(),
            P(),
            P("batch", None, None, "chan"),
        ),
        out_specs=(
            P("batch", None, None, "chan"),
            P("batch", None, None, "chan"),
            P(None, None, "chan"),
            P("chan"),
            P(),
            P(),
            P(),
            P(),
            P(),
            P(),
            P(),
        ),
        check_vma=False,
    )
```

```python
import functools

import jax
import jax.numpy as jnp
import numpy as np
from jax import lax
from jax.experimental import pallas as pl
from jax.experimental.pallas import tpu as pltpu
from jax.sharding import PartitionSpec as P

F32, BF16, I32 = jnp.float32, jnp.bfloat16, jnp.int32
MESH = pl.DeviceIdType.MESH
NT = (((1,), (1,)), ((), ()))
L = 128
ROOM, FULL = 15, 23
FACTOR = np.float32(1.0) / np.float32(0.9)
TAP = 21
SPAN = 384
BLOCK = 192


EDGE = 96
REACH = 9
MEGA = 1 << 20
QUARTERS = 4
AHEAD = 5
LAG = 0
ORDER = ("l", "h0", "H0", "h1", "z", "s1", "w", "a", "r0", "H1", "h2", "r1", "H2", "h3", "c0", "H3", "h4", "c1", "H4", "g4", "c2", "G4",
         "g3", "c3", "G3", "g2", "k", "i", "G2", "g1", "G1", "g0", "K", "G0")


def pieces(slots, step):
    return [(k, min(step, slots - k)) for k in range(0, slots, step)]


def gelu_parts(h):
    a = 1.0 + np.float32(0.3275911 / np.sqrt(2.0)) * jnp.abs(h)
    t = pl.reciprocal(a, approx=True)
    t = t * (2.0 - a * t)
    e = jnp.exp(-0.5 * h * h)
    c = [0.5 * v for v in (0.254829592, -0.284496736, 1.421413741, -1.453152027, 1.061405429)]
    q = t * (c[0] + t * (c[1] + t * (c[2] + t * (c[3] + t * c[4])))) * e
    cdf = jnp.where(h >= 0, 1.0 - q, q)
    return h * cdf, cdf + (np.float32(1 / np.sqrt(2 * np.pi)) * h) * e


def plan_kernel(side, mask_ref, keep_ref, rows_ref, cols_ref, wide_ref, perm_ref, permt_ref, off_ref, plo_ref):
    N = keep_ref.shape[1]
    wide = jnp.sum(mask_ref[0], axis=0, keepdims=True)
    key = jnp.where(keep_ref[...] > 0, 1 + (wide >= 18).astype(I32) + (wide >= 24).astype(I32), 0).astype(F32)
    wide_ref[...] = wide
    key = jnp.concatenate([key, jnp.zeros((1, L - N), F32)], axis=1)
    a = lax.broadcasted_iota(I32, (L, L), 0)
    b = lax.broadcasted_iota(I32, (L, L), 1)
    eye = a == b
    here = jnp.broadcast_to(key, (L, L))
    there = jnp.broadcast_to(jnp.sum(jnp.where(eye, here, 0.0), axis=1, keepdims=True), (L, L))
    ahead = ((there > here) | ((there == here) & (a < b))).astype(F32)
    rank = jnp.sum(ahead, axis=0, keepdims=True)
    behind = ((here > there) | ((here == there) & (b < a))).astype(F32)
    rank_col = jnp.sum(behind, axis=1, keepdims=True)
    permt_ref[...] = ((rank == a.astype(F32)) & (here > 0.5)).astype(BF16)
    perm_ref[...] = ((rank_col == b.astype(F32)) & (there > 0.5)).astype(BF16)
    counts = [jnp.sum((key > t).astype(F32), axis=1, keepdims=True) for t in (2.5, 1.5, 0.5)]
    strides = [jnp.maximum(c, 16.0) for c in counts]
    off = sum(s * rows_ref[i:i + 1, :] for i, s in enumerate(strides)) + rows_ref[3:4, :]
    for i, c in enumerate(counts):
        off = off + c * rows_ref[4 + i:5 + i, :]
    off_ref[...] = off.astype(I32)
    ends = sum(s * cols_ref[:, i:i + 1] for i, s in enumerate(strides)) + cols_ref[:, 3:4]
    start = lax.broadcasted_iota(I32, (1, plo_ref.shape[1]), 1).astype(F32) * float(L)
    plo_ref[...] = jnp.sum((ends <= start).astype(F32), axis=0, keepdims=True).astype(I32)


def plan(valid_mask, keep_mask):
    N, side, _ = valid_mask.shape
    places = side * side
    reach = np.maximum(*np.meshgrid(np.arange(side), np.arange(side), indexing="ij")).reshape(-1)
    rings = [reach >= 18, (reach >= 14) & (reach < 18), reach < 14]
    before = np.stack([np.concatenate([[0], np.cumsum(m)]) for m in rings]).astype(np.float32)
    rows = np.zeros((8, 640), np.float32)
    rows[0:3, :places + 1] = before
    rows[3, places + 1:600] = MEGA
    for i in range(3):
        rows[4 + i, 600 + i] = 1.0
    cols = np.zeros((640, 8), np.float32)
    cols[:places, 0:3] = before[:, 1:].T
    cols[places:, 3] = MEGA
    vm = pl.BlockSpec(memory_space=pltpu.VMEM)
    wide, perm, permt, off, plo = pl.pallas_call(
        functools.partial(plan_kernel, side),
        grid=(1,),
        out_shape=[jax.ShapeDtypeStruct((1, N), I32), jax.ShapeDtypeStruct((L, L), BF16), jax.ShapeDtypeStruct((L, L), BF16),
                   jax.ShapeDtypeStruct((1, 640), I32), jax.ShapeDtypeStruct((1, 512), I32)],
        in_specs=[pl.BlockSpec((1, side, N), lambda i: (0, 0, 0)), vm, vm, vm],
        out_specs=[vm] * 5,
        name="plan",
    )(jnp.transpose(valid_mask, (1, 2, 0)), keep_mask[None, :], rows, cols)
    return wide, perm, permt, off, plo


def main_kernel(cfg, plo, off, x_hbm, s_ref, cot_hbm, perm_ref, permt_ref, kern_ref, bias_ref, band_ref, w1_hbm, w2_hbm,
                gain_ref, shift_ref, b2_ref, scale_ref, wide_bias_ref,
                br_out, ig_out, rg_out, eg_out, small_out, kg_out, og_out,
                x_ref, cot_ref, w1_ref, w2_ref, w1t_ref, w2t_ref,
                xf, srt, xpad, cpad, tall, vecs, taps, flip, cols, b1_ref, bc_send, f_send, bc_recv, f_recv, fc_recv,
                rg_acc, eg_acc, vec_acc, wid_acc, res, hold, small, small_recv, kg_acc, og_acc, kg_recv, og_recv,
                ld_sem, in_ssem, in_rsem, out_ssem, out_rsem, st_sem, ex_ssem, ex_rsem, sm_ssem, sm_rsem, kg_ssem, kg_rsem):
    side, C, N, K, NC, step = cfg
    C2 = NC * C
    FF = w2_ref.shape[0]
    rows = side * C
    maps = side * side
    b = lax.axis_index("batch")
    me = lax.axis_index("chan")
    parts = pieces(K, step)

    cot_loads = [pltpu.make_async_copy(cot_hbm.at[pl.ds(j * side // QUARTERS, side // QUARTERS)],
                                       cot_ref.at[pl.ds(j * side // QUARTERS, side // QUARTERS)], ld_sem.at[j]) for j in range(QUARTERS)]
    x_loads = [pltpu.make_async_copy(x_hbm.at[pl.ds(j * side // QUARTERS, side // QUARTERS)],
                                     x_ref.at[pl.ds(j * side // QUARTERS, side // QUARTERS)], ld_sem.at[QUARTERS + j]) for j in range(QUARTERS)]
    w_loads = [pltpu.make_async_copy(s, d, ld_sem.at[2 * QUARTERS + i]) for i, (s, d) in enumerate(((w1_hbm, w1_ref), (w2_hbm, w2_ref)))]
    for cp in cot_loads:
        cp.start()

    bar = pltpu.get_barrier_semaphore()
    def greet(m, _):
        pl.semaphore_signal(bar, inc=1, device_id=(b, lax.rem(me + m, NC)), device_id_type=MESH)
        return 0
    lax.fori_loop(1, NC, greet, 0)
    pl.semaphore_signal(bar, inc=1, device_id=(1 - b, me), device_id_type=MESH)

    lane = lax.broadcasted_iota(I32, (C, L), 1)
    perm = perm_ref[...]
    permt = permt_ref[...]
    s = s_ref[...]

    def send(src, dst, s0, n, ssem, rsem, part=None):
        if part == "column":
            return column(src, dst, s0, n, ssem, rsem)
        sl = pl.ds(s0, n)
        def one(m, _):
            t = lax.rem(me + m, NC)
            pltpu.make_async_remote_copy(
                src_ref=src.at[sl, t], dst_ref=dst.at[sl, me], send_sem=ssem, recv_sem=rsem,
                device_id=(b, t), device_id_type=MESH).start()
            return 0
        if part is None:
            lax.fori_loop(1, NC, one, 0)
        else:
            for m in range(1, NC):
                if m % 4:
                    one(m, 0)
        pltpu.make_async_copy(src.at[sl, me], dst.at[sl, me], rsem).start()

    def column(src, dst, s0, n, ssem, rsem):
        sl = pl.ds(s0, n)
        for m in range(4, NC, 4):
            t = lax.rem(me + m, NC)
            pltpu.make_async_remote_copy(
                src_ref=src.at[sl, t], dst_ref=dst.at[sl, me], send_sem=ssem, recv_sem=rsem,
                device_id=(b, t), device_id_type=MESH).start()

    def arrived(dst, s0, n, rsem):
        ref = dst.at[pl.ds(s0, n)]
        pltpu.make_async_copy(ref, ref, rsem).wait()

    def sent(src, ssem):
        ref = src.at[:, pl.ds(0, NC - 1)]
        pltpu.make_async_copy(ref, ref, ssem).wait()

    def pack(dst, s0, n):
        def group(g):
            p0 = plo[0, g]
            acc = jnp.zeros((C, L), F32)
            for t in range(REACH):
                sh = off[0, p0 + t] - g * L
                v = srt[p0 + t]
                acc = jnp.where(lane >= sh, pltpu.roll(v, lax.bitwise_and(sh, L - 1), 1), acc)
            return acc
        B = 8
        def body(h, _):
            sl = s0 + h * B // NC
            d0 = lax.rem(h * B, NC)
            accs = [group(sl * NC + d0 + i) for i in range(B)]
            for i in range(B):
                dst[sl, d0 + i] = accs[i].astype(BF16)
            return 0
        lax.fori_loop(0, n * NC // B, body, 0, unroll=2)

    def unpack(src, i, j):
        p = i * side + j
        o = off[0, p]
        g = lax.shift_right_logical(o, 7)
        r = lax.bitwise_and(o, L - 1)
        g2 = jnp.minimum(g + 1, K * NC - 1)
        a = src[lax.shift_right_logical(g, 4), lax.bitwise_and(g, NC - 1)].astype(F32)
        v = src[lax.shift_right_logical(g2, 4), lax.bitwise_and(g2, NC - 1)].astype(F32)
        v = jnp.where(lane >= r, a, v)
        v = pltpu.roll(v, lax.bitwise_and(L - r, L - 1), 1)
        m = jnp.maximum(i, j)
        n = jnp.where(m < 14, off[0, 602], jnp.where(m < 18, off[0, 601], off[0, 600]))
        return jnp.where(lane < n, v, 0.0)

    srt[maps] = jnp.zeros((C, L), F32)
    def bc_row(i, _):
        vals = []
        for j in range(side):
            m = jnp.where(s > jnp.maximum(i, j), FACTOR, F32(0.0))
            vals.append(cot_ref[i, j].astype(F32) * m)
        v = jnp.concatenate(vals, axis=0).astype(BF16)
        srt[pl.ds(i * side, side)] = jnp.dot(v, perm_ref[0:N, :], preferred_element_type=F32).reshape(side, C, L)
        return 0
    for j, cp in enumerate(cot_loads):
        cp.wait()
        lax.fori_loop(j * side // QUARTERS, (j + 1) * side // QUARTERS, bc_row, 0)
    for cp in x_loads:
        cp.start()
    pl.semaphore_wait(bar, NC)
    for k, (s0, n) in enumerate(parts):
        pack(bc_send, s0, n)
        send(bc_send, bc_recv, s0, n, in_ssem.at[0], in_rsem.at[0, k])

    for cp in w_loads:
        cp.start()
    tall[...] = jnp.zeros_like(tall)
    ks = kern_ref.shape[0]
    for a in range(ks):
        row = kern_ref[a].astype(F32)
        at = TAP + a * side
        tall[0, at:at + ks, 0:C] = row
        at = TAP + (ks - 1 - a) * side
        for i in range(ks):
            tall[1, at + ks - 1 - i:at + ks - i, 0:C] = row[i:i + 1, :]
    taps[...] = jnp.transpose(tall[0])[0:C, :]
    flip[...] = jnp.transpose(tall[1])[0:C, :]
    def x_row(i, _):
        for j in range(side):
            m = (s > jnp.maximum(i, j)).astype(F32)
            xf[pl.ds(pl.multiple_of(i * rows + j * C, 8), C), 0:N] = x_ref[i, j].astype(F32) * m
        return 0
    xpad[...] = jnp.zeros_like(xpad)
    for j, cp in enumerate(x_loads):
        cp.wait()
        lax.fori_loop(j * side // QUARTERS, (j + 1) * side // QUARTERS, x_row, 0)

    def banded(tap, win):
        tap = jnp.broadcast_to(tap, (8, SPAN))
        tiles = [pltpu.roll(tap, 8 * k, 1, stride=1, stride_axis=0) * band_ref[8 * k:8 * k + 8, :] for k in range(BLOCK // 8)]
        return jnp.dot(jnp.concatenate(tiles, axis=0).astype(BF16), win, preferred_element_type=F32)

    def windows(pad, c):
        return jnp.concatenate([pad[c, BLOCK * g:BLOCK * g + SPAN, :] for g in range(maps // BLOCK)], axis=1)

    def spread(c, out):
        for g in range(maps // BLOCK):
            xf[pl.ds(g * BLOCK * C + c, BLOCK, stride=C), :] = out[:, g * L:(g + 1) * L]

    def channel(c, _):
        xpad[c, EDGE:EDGE + maps, 0:N] = xf[pl.ds(c, maps, stride=C), :][:, 0:N].astype(BF16)
        spread(c, banded(taps[pl.ds(c, 1), :], windows(xpad, c)))
        return 0
    lax.fori_loop(0, C, channel, 0)

    vecs[...] = jnp.zeros_like(vecs)
    vecs[8:9, 0:C] = bias_ref[...].astype(F32).reshape(1, C)
    for i, ref in enumerate((gain_ref, shift_ref, b2_ref, scale_ref)):
        vecs[i:i + 1, :] = ref[...].astype(F32).reshape(1, C2)
    for i in range(FF // C2):
        vecs[4 + i:5 + i, :] = wide_bias_ref[i * C2:(i + 1) * C2].astype(F32).reshape(1, C2)
    turned = jnp.transpose(vecs[...])
    bias = jnp.concatenate([jnp.broadcast_to(turned[0:C, 8:9], (C, L))] * side, axis=0)
    def f_row(i, _):
        v = (xf[pl.ds(pl.multiple_of(i * rows, 8), rows), :] + bias).astype(BF16)
        srt[pl.ds(i * side, side)] = jnp.dot(v, perm, preferred_element_type=F32).reshape(side, C, L)
        return 0
    lax.fori_loop(0, side, f_row, 0)
    for k, (s0, n) in enumerate(parts):
        pack(f_send, s0, n)
        if k < AHEAD:
            send(f_send, f_recv, s0, n, in_ssem.at[1], in_rsem.at[1, k])

    for cp in w_loads:
        cp.wait()
    w1t_ref[...] = jnp.transpose(w1_ref[...])
    w2t_ref[...] = jnp.transpose(w2_ref[...])
    cols[...] = turned
    for i in range(FF // C2):
        b1_ref[i * C2:(i + 1) * C2, :] = turned[:, 4 + i:5 + i]
    rg_acc[...] = jnp.zeros_like(rg_acc)
    eg_acc[...] = jnp.zeros_like(eg_acc)
    vec_acc[...] = jnp.zeros_like(vec_acc)
    wid_acc[...] = jnp.zeros_like(wid_acc)
    FB = 256
    whole = K // step


    def feed(k):
        if isinstance(k, int):
            if k + AHEAD < len(parts):
                s0, n = parts[k + AHEAD]
                send(f_send, f_recv, s0, n, in_ssem.at[1], in_rsem.at[1, k + AHEAD])
            return
        @pl.when(k + AHEAD < whole)
        def _():
            send(f_send, f_recv, (k + AHEAD) * step, step, in_ssem.at[1], in_rsem.at[1, k + AHEAD])
        for j in range(whole, len(parts)):
            @pl.when(k + AHEAD == j)
            def _():
                send(f_send, f_recv, parts[j][0], parts[j][1], in_ssem.at[1], in_rsem.at[1, j])

    def mlp(s0, n, k):
        W = n * L

        def fold(v):
            out = v[:, 0:L]
            for t in range(1, n):
                out = out + v[:, t * L:(t + 1) * L]
            return out

        def load(ref):
            return jnp.concatenate([ref[s0 + t].astype(F32).reshape(C2, L) for t in range(n)], axis=1)

        def store(ref, v):
            for t in range(n):
                ref[s0 + t] = v[:, t * L:(t + 1) * L].reshape(NC, C, L).astype(BF16)

        arrived(bc_recv, s0, n, in_rsem.at[0, k])
        arrived(f_recv, s0, n, in_rsem.at[1, k])
        feed(k)
        gain, shift, b2, scale = (cols[:, i:i + 1] for i in range(4))
        f = load(f_recv)
        d = f - jnp.mean(f, axis=0, keepdims=True)
        inv = lax.rsqrt(jnp.mean(d * d, axis=0, keepdims=True) + 1e-6)
        xhat = d * inv
        normed = (xhat * gain + shift).astype(BF16)
        bc = load(bc_recv)
        rc = (scale * bc).astype(BF16)
        vec_acc[2] += fold(rc.astype(F32))
        red = jnp.zeros((C2, W), F32)
        nc = jnp.zeros((C2, W), F32)
        for fb in range(FF // FB):
            r = slice(fb * FB, (fb + 1) * FB)
            h = jnp.dot(w1t_ref[r, :], normed, preferred_element_type=F32) + b1_ref[r, :]
            act, slope = gelu_parts(h)
            act = act.astype(BF16)
            ac = jnp.dot(w2_ref[r, :], rc, preferred_element_type=F32)
            hc = (ac * slope).astype(BF16)
            red = red + jnp.dot(w2t_ref[:, r], act, preferred_element_type=F32)
            nc = nc + jnp.dot(w1_ref[:, r], hc, preferred_element_type=F32)
            rg_acc[r, :] += lax.dot_general(act, rc, NT, preferred_element_type=F32)
            eg_acc[r, :] += lax.dot_general(hc, normed, NT, preferred_element_type=F32)
            wid_acc[r, :] += fold(hc.astype(F32))
        red = red + b2
        store(bc_recv, scale * red)
        vec_acc[3] += fold(bc * red)
        vec_acc[0] += fold(nc * xhat)
        vec_acc[1] += fold(nc)
        q = nc * gain
        m1 = jnp.mean(q, axis=0, keepdims=True)
        m2 = jnp.mean(q * xhat, axis=0, keepdims=True)
        store(f_recv, inv * (q - m1 - xhat * m2))

    def mlp_step(k, _):
        mlp(k * step, step, k)
        @pl.when(k >= LAG)
        def _():
            j = k - LAG
            send(f_recv, fc_recv, j * step, step, out_ssem.at[0], out_rsem.at[0, j])
        return 0
    lax.fori_loop(0, whole, mlp_step, 0)
    for k, (s0, n) in list(enumerate(parts))[whole:]:
        mlp(s0, n, k)


    ones = jnp.ones((8, L), F32)
    def row_of(v):
        return lax.dot_general(ones, v, NT, precision=lax.Precision.HIGHEST, preferred_element_type=F32)
    sub = lax.broadcasted_iota(I32, (8, C2), 0)
    tot = jnp.zeros((8, C2), F32)
    for i in range(4):
        tot = tot + jnp.where(sub == i, row_of(vec_acc[i]), 0.0)
    for i in range(FF // C2):
        tot = tot + jnp.where(sub == 4 + i, row_of(wid_acc[i * C2:(i + 1) * C2, :]), 0.0)
    over = jnp.where(off[0, maps] > K * NC * L, F32(1.0), F32(0.0))
    small[0:8, :] = tot
    small[8:16, :] = jnp.zeros((8, C2), F32) + over

    accs, outs = (rg_acc, eg_acc), (rg_out, eg_out)
    def peer(bit):
        if bit < 0:
            return (1 - b, me), b
        w = 1 << bit
        on = lax.rem(me // w, 2)
        return (b, me + w - 2 * w * on), on
    orders = ((-1, -1), (0, 1), (1, 0), (2, 2), (3, 3))
    base = [0, 0]
    legs = []
    lo, span = 0, FF
    for st, bits in enumerate(orders):
        span //= 2
        leg = []
        for a in range(2):
            dev, on = peer(bits[a])
            theirs = pl.multiple_of(base[a] + (1 - on) * span, 16)
            base[a] = pl.multiple_of(base[a] + on * span, 16)
            cp = pltpu.make_async_remote_copy(
                src_ref=hold.at[a, pl.ds(0, span)], dst_ref=res.at[a, pl.ds(lo, span)],
                send_sem=ex_ssem.at[a, st], recv_sem=ex_rsem.at[a, st], device_id=dev, device_id_type=MESH)
            leg.append((cp, theirs, base[a], dev))
        dev, _ = peer(bits[0])
        sc = pltpu.make_async_remote_copy(
            src_ref=small, dst_ref=small_recv.at[st], send_sem=sm_ssem.at[st], recv_sem=sm_rsem.at[st],
            device_id=dev, device_id_type=MESH)
        legs.append((lo, span, leg, sc))
        lo += span

    def halve_start(st):
        lo, span, leg, sc = legs[st]
        for a in range(2):
            cp, theirs, _, _ = leg[a]
            hold[a, 0:span, :] = accs[a][pl.ds(theirs, span), :].astype(BF16)
            cp.start()
        sc.start()

    def halve_end(st):
        lo, span, leg, sc = legs[st]
        for a in range(2):
            cp, _, mine, _ = leg[a]
            cp.wait()
            accs[a][pl.ds(mine, span), :] += res[a, lo:lo + span, :].astype(F32)
        sc.wait()
        small[...] += small_recv[st]

    back = {}
    def gather_start(st):
        lo, span, leg, _ = legs[st]
        back[st] = []
        for a in range(2):
            ref = outs[a].at[pl.ds(leg[a][2], span)]
            cp = pltpu.make_async_remote_copy(
                src_ref=ref, dst_ref=ref, send_sem=ex_ssem.at[a, 5 + st], recv_sem=ex_rsem.at[a, 5 + st],
                device_id=leg[a][3], device_id_type=MESH)
            cp.start()
            back[st].append(cp)

    def gather_end(st):
        for cp in back[st]:
            cp.wait()

    def bulk(kind, k, part=None):
        s0, n = parts[k]
        if kind == 1 and part is None:
            part = "others"
        src, dst = ((f_recv, fc_recv), (bc_recv, br_out))[kind]
        send(src, dst, s0, n, out_ssem.at[kind], out_rsem.at[kind, k], part)

    late = [(0, k) for k in range(max(whole - LAG, 0), len(parts))]
    todo = late + [(1, k) for k in range(len(parts))]
    def some(share):
        for _ in range(min(share, len(todo))):
            bulk(*todo.pop(0))

    def fc_row(i, _):
        vals = [unpack(fc_recv, i, j) for j in range(side)]
        tot = vals[0]
        for v in vals[1:]:
            tot = tot + v
        og_acc[...] += tot
        v = jnp.concatenate(vals, axis=0).astype(BF16)
        xf[pl.ds(pl.multiple_of(i * rows, 8), rows), :] = jnp.dot(v, permt, preferred_element_type=F32)
        return 0

    def channel_back(c, _):
        cpad[c, EDGE:EDGE + maps, :] = xf[pl.ds(c, maps, stride=C), :].astype(BF16)
        spread(c, banded(flip[pl.ds(c, 1), :], windows(cpad, c)))
        mid = jnp.concatenate([cpad[c, EDGE + BLOCK * g:EDGE + BLOCK * (g + 1), :] for g in range(maps // BLOCK)], axis=1)
        gram = lax.dot_general(mid, windows(xpad, c), NT, preferred_element_type=F32) * band_ref[...]
        acc = jnp.zeros((8, SPAN), F32)
        for k in range(BLOCK // 8):
            acc = acc + pltpu.roll(gram[8 * k:8 * k + 8, :], (SPAN - 8 * k) % SPAN, 1)
        kg_acc[c] = acc
        return 0

    swap = [pltpu.make_async_remote_copy(src_ref=v, dst_ref=r, send_sem=kg_ssem.at[i], recv_sem=kg_rsem.at[i],
                                         device_id=(1 - b, me), device_id_type=MESH)
            for i, (v, r) in enumerate(((kg_acc, kg_recv), (og_acc, og_recv)))]

    def ig_row(i, _):
        for j in range(side):
            m = (s > jnp.maximum(i, j)).astype(F32)
            v = xf[pl.ds(pl.multiple_of(i * rows + j * C, 8), C), :][:, 0:N]
            x_ref[i, j] = (cot_ref[i, j].astype(F32) + v * m).astype(BF16)
        return 0

    put = pltpu.make_async_copy(x_ref, ig_out, st_sem)

    def share(n, of, body, total):
        lax.fori_loop(n * total // of, (n + 1) * total // of, body, 0)

    cpad[...] = jnp.zeros_like(cpad)
    og_acc[...] = jnp.zeros_like(og_acc)
    for word in ORDER:
        op, num = word[0], int(word[1:] or 0)
        if op == "h":
            halve_start(num)
        elif op == "H":
            halve_end(num)
            if num == 4:
                small_out[...] = small[...]
                for a in range(2):
                    mine = legs[4][2][a][2]
                    outs[a][pl.ds(mine, legs[4][1]), :] = accs[a][pl.ds(mine, legs[4][1]), :].astype(BF16)
        elif op == "g":
            gather_start(num)
        elif op == "G":
            gather_end(num)
        elif op == "s":
            some(num)
        elif op == "z":
            for k in range(len(parts)):
                bulk(1, k, "column")
        elif op == "a":
            some(len(todo))
        elif op == "l":
            while todo[0][0] == 0:
                some(1)
        elif op == "w":
            for k, (s0, n) in enumerate(parts):
                arrived(fc_recv, s0, n, out_rsem.at[0, k])
        elif op == "r":
            share(num, 2, fc_row, side)
        elif op == "c":
            share(num, 4, channel_back, C)
        elif op == "k":
            for cp in swap:
                cp.start()
        elif op == "K":
            for cp in swap:
                cp.wait()
            kg_out[...] = kg_acc[...] + kg_recv[...]
            og_out[...] = og_acc[...] + og_recv[...]
        elif op == "i":
            share(0, 1, ig_row, side)
            put.start()

    put.wait()
    for k, (s0, n) in enumerate(parts):
        arrived(br_out, s0, n, out_rsem.at[1, k])
    sent(bc_send, in_ssem.at[0])
    sent(f_send, in_ssem.at[1])
    sent(f_recv, out_ssem.at[0])
    sent(bc_recv, out_ssem.at[1])


def tail_kernel(cfg, off, x_hbm, permt_ref, br_hbm, ig_hbm, rg_hbm, eg_hbm, small_ref, kg_ref, og_ref,
                out_hbm, ig_out, rg_out, eg_out, kg_out, og_out, wide_out, over_out, *rest):
    side, C, N, K, NC, _ = cfg
    vec_outs = rest[:4]
    x_ref, br_ref, ig_ref, rg_ref, eg_ref, rg_f, eg_f, sem = rest[4:]
    lane = lax.broadcasted_iota(I32, (C, L), 1)
    ks = kg_out.shape[0]
    C2 = small_ref.shape[1]
    br_in = pltpu.make_async_copy(br_hbm, br_ref, sem.at[0])
    rg_in = pltpu.make_async_copy(rg_hbm, rg_ref, sem.at[1])
    eg_in = pltpu.make_async_copy(eg_hbm, eg_ref, sem.at[2])
    ig_in = pltpu.make_async_copy(ig_hbm, ig_ref, sem.at[3])
    x_in = [pltpu.make_async_copy(x_hbm.at[pl.ds(j * side // QUARTERS, side // QUARTERS)],
                                  x_ref.at[pl.ds(j * side // QUARTERS, side // QUARTERS)], sem.at[8 + j]) for j in range(QUARTERS)]
    br_in.start()
    for cp in x_in:
        cp.start()
    rg_in.start()
    eg_in.start()
    ig_in.start()
    permt = permt_ref[...]

    def unpack(i, j):
        o = off[0, i * side + j]
        g = lax.shift_right_logical(o, 7)
        r = lax.bitwise_and(o, L - 1)
        v = jnp.where(lane >= r, br_ref[g].astype(F32), br_ref[jnp.minimum(g + 1, K * NC - 1)].astype(F32))
        v = pltpu.roll(v, lax.bitwise_and(L - r, L - 1), 1)
        m = jnp.maximum(i, j)
        n = jnp.where(m < 14, off[0, 602], jnp.where(m < 18, off[0, 601], off[0, 600]))
        return jnp.where(lane < n, v, 0.0)

    def br_row(i, _):
        v = jnp.concatenate([unpack(i, j) for j in range(side)], axis=0).astype(BF16)
        v = jnp.dot(v, permt, preferred_element_type=F32)
        for j in range(side):
            x_ref[i, j] = (x_ref[i, j].astype(F32) + FACTOR * v[j * C:(j + 1) * C, 0:N]).astype(BF16)
        return 0

    br_in.wait()
    x_out = []
    for j, cp in enumerate(x_in):
        cp.wait()
        sl = pl.ds(j * side // QUARTERS, side // QUARTERS)
        lax.fori_loop(j * side // QUARTERS, (j + 1) * side // QUARTERS, br_row, 0, unroll=2)
        put = pltpu.make_async_copy(x_ref.at[sl], out_hbm.at[sl], sem.at[12 + j])
        put.start()
        x_out.append(put)
        if j == 0:
            ig_in.wait()
            put = pltpu.make_async_copy(ig_ref, ig_out, sem.at[4])
            put.start()
            x_out.append(put)
        if j == 1:
            rg_in.wait()
            rg_f[...] = rg_ref[...].astype(F32)
            put = pltpu.make_async_copy(rg_f, rg_out, sem.at[5])
            put.start()
            x_out.append(put)
        if j == 2:
            eg_in.wait()
            eg_f[...] = jnp.transpose(eg_ref[...].astype(F32))
            put = pltpu.make_async_copy(eg_f, eg_out, sem.at[6])
            put.start()
            x_out.append(put)

    total = kg_ref[:, 0, :]
    for q in range(1, 8):
        total = total + pltpu.roll(kg_ref[:, q, :], SPAN - q, 1)
    turned = jnp.transpose(total)
    for a in range(ks):
        kg_out[a] = turned[TAP + a * side:TAP + a * side + ks, :]
    og_out[...] = jnp.sum(jnp.transpose(og_ref[...]), axis=0)
    for i, ref in enumerate(vec_outs):
        ref[...] = small_ref[i, :]
    for i in range(wide_out.shape[0] // C2):
        wide_out[i * C2:(i + 1) * C2] = small_ref[4 + i, :]
    over_out[...] = small_ref[8, 0:L]
    for put in x_out:
        put.wait()


def packed_form(K, step, cid, inputs, kernel, offset, norm_gain, norm_shift, expand_weight, expand_offset, reduce_weight, reduce_offset,
                layer_scale, cotangent, wide, perm, permt, off, plo):
    N, side, _, C = inputs.shape
    C2, FF = expand_weight.shape
    NC = C2 // C
    cfg = (side, C, N, K, NC, step)
    ks = kernel.shape[0]
    x = jnp.transpose(inputs, (1, 2, 3, 0))
    cot = jnp.transpose(cotangent, (1, 2, 3, 0))
    r = np.arange(BLOCK)
    l = np.arange(SPAN)
    band = (np.abs(l[None] % side - r[:, None] % side) <= ks // 2).astype(np.float32)
    vm = pl.BlockSpec(memory_space=pltpu.VMEM)
    sm = pl.BlockSpec(memory_space=pltpu.SMEM)
    hbm = pl.BlockSpec(memory_space=pl.ANY)
    blk = (K, NC, C, L)
    img = (side, side, C, N)
    steps = len(pieces(K, step))
    held = FF - FF // 32
    sd = jax.ShapeDtypeStruct
    dma = pltpu.SemaphoreType.DMA
    br, ig, rg, eg, small, kg, og = pl.pallas_call(
        functools.partial(main_kernel, cfg),
        out_shape=[sd(blk, BF16), sd(img, BF16), sd((FF, C2), BF16), sd((FF, C2), BF16), sd((16, C2), F32),
                   sd((C, 8, SPAN), F32), sd((C, L), F32)],
        in_specs=[sm, sm, hbm, vm, hbm, vm, vm, vm, vm, vm, hbm, hbm] + [vm] * 5,
        out_specs=[hbm, hbm, vm, vm, vm, vm, vm],
        scratch_shapes=[
            pltpu.VMEM(img, BF16), pltpu.VMEM(img, BF16),
            pltpu.VMEM((C2, FF), BF16), pltpu.VMEM((FF, C2), BF16), pltpu.VMEM((FF, C2), BF16), pltpu.VMEM((C2, FF), BF16),
            pltpu.VMEM((side * side * C, L), F32), pltpu.VMEM((586, C, L), F32),
            pltpu.VMEM((C, 768, L), BF16), pltpu.VMEM((C, 768, L), BF16),
            pltpu.VMEM((2, SPAN, L), F32), pltpu.VMEM((16, C2), F32),
            pltpu.VMEM((C, SPAN), F32), pltpu.VMEM((C, SPAN), F32), pltpu.VMEM((C2, 16), F32), pltpu.VMEM((FF, 1), F32),
            pltpu.VMEM(blk, BF16), pltpu.VMEM(blk, BF16), pltpu.VMEM(blk, BF16), pltpu.VMEM(blk, BF16), pltpu.VMEM(blk, BF16),
            pltpu.VMEM((FF, C2), F32), pltpu.VMEM((FF, C2), F32), pltpu.VMEM((4, C2, L), F32), pltpu.VMEM((FF, L), F32),
            pltpu.VMEM((2, held, C2), BF16), pltpu.VMEM((2, FF // 2, C2), BF16),
            pltpu.VMEM((16, C2), F32), pltpu.VMEM((5, 16, C2), F32),
            pltpu.VMEM((C, 8, SPAN), F32), pltpu.VMEM((C, L), F32), pltpu.VMEM((C, 8, SPAN), F32), pltpu.VMEM((C, L), F32),
            dma((2 * QUARTERS + 2,)), dma((2,)), dma((2, steps)), dma((2,)), dma((2, steps)), dma,
            dma((2, 10)), dma((2, 10)), dma((5,)), dma((5,)), dma((2,)), dma((2,)),
        ],
        compiler_params=pltpu.CompilerParams(collective_id=cid, has_side_effects=True, vmem_limit_bytes=63 << 20),
        name="main_%d" % K,
    )(plo, off, x, wide, cot, perm, permt, kernel, offset, band, expand_weight, reduce_weight,
      norm_gain, norm_shift, reduce_offset, layer_scale, expand_offset)
    row = sd((C2,), F32)
    out, ig, rg, eg, kg, og, widen, over, gain, shift, narrow, scale = pl.pallas_call(
        functools.partial(tail_kernel, cfg),
        out_shape=[sd(img, BF16), sd(img, BF16), sd((FF, C2), F32), sd((C2, FF), F32), sd((ks, ks, C), F32), sd((C,), F32),
                   sd((FF,), F32), sd((L,), F32), row, row, row, row],
        in_specs=[sm, hbm, vm, hbm, hbm, hbm, hbm, vm, vm, vm],
        out_specs=[hbm] * 4 + [vm] * 8,
        scratch_shapes=[pltpu.VMEM(img, BF16), pltpu.VMEM((K * NC, C, L), BF16), pltpu.VMEM(img, BF16), pltpu.VMEM((FF, C2), BF16),
                        pltpu.VMEM((FF, C2), BF16), pltpu.VMEM((FF, C2), F32), pltpu.VMEM((C2, FF), F32), dma((16,))],
        compiler_params=pltpu.CompilerParams(vmem_limit_bytes=60 << 20),
        name="tail_%d" % K,
    )(off, x, permt, br.reshape(K * NC, C, L), ig, rg, eg, small, kg, og)
    return (jnp.transpose(out, (3, 0, 1, 2)), jnp.transpose(ig, (3, 0, 1, 2)), kg, og, gain, shift, eg, widen, rg, narrow, scale), over


keep_rate = 0.9
epsilon = 1e-06


def exact_gelu(values):
    return jax.nn.gelu(values, approximate=False)


def layer_norm(values, gain, shift):
    center = jnp.mean(values, axis=-1, keepdims=True)
    spread = jnp.mean(jnp.square(values - center), axis=-1, keepdims=True)
    return (values - center) * lax.rsqrt(spread + epsilon) * gain + shift


def dense_form(
    inputs,
    valid_mask,
    keep_mask,
    kernel,
    offset,
    norm_gain,
    norm_shift,
    expand_weight,
    expand_offset,
    reduce_weight,
    reduce_offset,
    layer_scale,
    cotangent,
):
    images, height, breadth, channels = inputs.shape
    kside = kernel.shape[0]
    pixels = images * height * breadth
    mask_f = valid_mask.astype(jnp.float32)
    factor = mask_f * (keep_mask.astype(jnp.float32) / keep_rate)[:, None, None]

    def local_conv(source, kern):
        return lax.conv_general_dilated(
            source,
            kern.reshape(kside, kside, 1, channels),
            (1, 1),
            "SAME",
            dimension_numbers=("NHWC", "HWIO", "NHWC"),
            feature_group_count=channels,
            precision=lax.Precision.HIGHEST,
        )

    masked = inputs.astype(jnp.float32) * mask_f[..., None]
    conv_out, conv_pull = jax.vjp(local_conv, masked, kernel.astype(jnp.float32))
    filtered = ((conv_out + offset.astype(jnp.float32)) * mask_f[..., None]).astype(jnp.bfloat16)
    flat_filtered = filtered.reshape(pixels, channels)
    pixel_rows = lax.all_to_all(flat_filtered, "chan", split_axis=0, concat_axis=1, tiled=True)
    normed_f, norm_pull = jax.vjp(
        layer_norm,
        pixel_rows.astype(jnp.float32),
        norm_gain.astype(jnp.float32),
        norm_shift.astype(jnp.float32),
    )
    normed = normed_f.astype(jnp.bfloat16)
    hidden = jnp.dot(
        normed, expand_weight, preferred_element_type=jnp.float32
    ) + expand_offset.astype(jnp.float32)
    active_f, gelu_pull = jax.vjp(exact_gelu, hidden)
    active = active_f.astype(jnp.bfloat16)
    reduced = jnp.dot(
        active, reduce_weight, preferred_element_type=jnp.float32
    ) + reduce_offset.astype(jnp.float32)
    scale_f = layer_scale.astype(jnp.float32)
    branch = (scale_f * reduced).astype(jnp.bfloat16)
    branch_back = lax.all_to_all(branch, "chan", split_axis=1, concat_axis=0, tiled=True)
    block_output = inputs.astype(jnp.float32) + factor[..., None] * branch_back.reshape(
        inputs.shape
    ).astype(jnp.float32)
    local_cot = (
        (cotangent.astype(jnp.float32) * factor[..., None])
        .astype(jnp.bfloat16)
        .reshape(pixels, channels)
    )
    branch_cot = lax.all_to_all(local_cot, "chan", split_axis=0, concat_axis=1, tiled=True)
    branch_cot_f = branch_cot.astype(jnp.float32)
    scale_sum = jnp.sum(branch_cot_f * reduced, axis=0)
    reduced_cot = (scale_f * branch_cot_f).astype(jnp.bfloat16)
    narrow_sum = jnp.sum(reduced_cot.astype(jnp.float32), axis=0)
    reduce_sum = jnp.einsum("pf,pc->fc", active, reduced_cot, preferred_element_type=jnp.float32)
    active_cot = jnp.einsum(
        "pc,fc->pf", reduced_cot, reduce_weight, preferred_element_type=jnp.float32
    )
    (hidden_cot_f,) = gelu_pull(active_cot)
    hidden_cot = hidden_cot_f.astype(jnp.bfloat16)
    widen_sum = jnp.sum(hidden_cot.astype(jnp.float32), axis=0)
    expand_sum = jnp.einsum("pc,pf->cf", normed, hidden_cot, preferred_element_type=jnp.float32)
    normed_cot = jnp.einsum(
        "pf,cf->pc", hidden_cot, expand_weight, preferred_element_type=jnp.float32
    )
    filtered_cot, gain_sum, shift_sum = norm_pull(normed_cot)
    filtered_back = lax.all_to_all(
        filtered_cot.astype(jnp.bfloat16), "chan", split_axis=1, concat_axis=0, tiled=True
    )
    conv_cot = filtered_back.reshape(inputs.shape).astype(jnp.float32) * mask_f[..., None]
    offset_sum = jnp.sum(conv_cot, axis=(0, 1, 2))
    masked_cot, kernel_sum = conv_pull(conv_cot)
    input_gradient = cotangent.astype(jnp.float32) + masked_cot * mask_f[..., None]
    kernel_total, offset_total = lax.psum((kernel_sum, offset_sum), "batch")
    expand_total, widen_total, reduce_total, narrow_total, scale_total, gain_total, shift_total = (
        lax.psum(
            (expand_sum, widen_sum, reduce_sum, narrow_sum, scale_sum, gain_sum, shift_sum),
            ("batch", "chan"),
        )
    )
    return (
        block_output.astype(jnp.bfloat16),
        input_gradient.astype(jnp.bfloat16),
        kernel_total,
        offset_total,
        gain_total,
        shift_total,
        expand_total,
        widen_total,
        reduce_total,
        narrow_total,
        scale_total,
    )


def per_device(inputs, valid_mask, keep_mask, kernel, offset, norm_gain, norm_shift, expand_weight, expand_offset, reduce_weight,
               reduce_offset, layer_scale, cotangent):
    images, side, _, channels = inputs.shape
    peers = expand_weight.shape[0] // channels
    if not (peers == 16 and channels % 8 == 0 and side == 24 and kernel.shape[0] == 7 and images <= L):
        return dense_form(inputs, valid_mask, keep_mask, kernel, offset, norm_gain, norm_shift, expand_weight, expand_offset,
                          reduce_weight, reduce_offset, layer_scale, cotangent)
    args = (inputs, kernel, offset, norm_gain, norm_shift, expand_weight, expand_offset, reduce_weight, reduce_offset, layer_scale,
            cotangent) + tuple(plan(valid_mask, keep_mask))
    outs, over = packed_form(ROOM, 2, 1, *args)
    again = lambda state: (packed_form(FULL, 1, 2, *args)[0], jnp.zeros((L,), F32))
    return lax.while_loop(lambda state: state[1][0] > 0.5, again, (outs, over))[0]


def solution(mesh):
    return jax.shard_map(
        per_device,
        mesh=mesh,
        in_specs=(
            P("batch", None, None, "chan"),
            P("batch", None, None),
            P("batch"),
            P(None, None, "chan"),
            P("chan"),
            P(),
            P(),
            P(),
            P(),
            P(),
            P(),
            P(),
            P("batch", None, None, "chan"),
        ),
        out_specs=(
            P("batch", None, None, "chan"),
            P("batch", None, None, "chan"),
            P(None, None, "chan"),
            P("chan"),
            P(),
            P(),
            P(),
            P(),
            P(),
            P(),
            P(),
        ),
        check_vma=False,
    )
```
